128 devices in a mesh: gx: 16 (over x, y), gy: 8 (over z, core).
Axes of the slice: x: 4, y: 4, z: 4, core: 2. Of those that a mesh axis runs over, the one named last changes fastest.
Arguments:
- hydro_old: float32 [8, 144, 27, 4096], P('gy', 'gx'), may hold values from -0.8 to 0.8
- phase_old: float32 [8, 144, 15, 4096], P('gy', 'gx'), may hold values from -0.8 to 0.8
- targets: int32 [8, 144], P('gy', 'gx'), may hold values from -1 to 127, as said below
- flags: int32 [8, 144], P('gy', 'gx'), may hold values 0 or 1
- relax_rates: float32 [27], replicated, may hold values from 0.8 to 1.8
Outputs:
- hydro_next: float32 [27, 256, 128, 128], P(None, 'gx', 'gy')
- phase_next: float32 [15, 256, 128, 128], P(None, 'gx', 'gy')
The draws below stay inside these ranges and needn't reach their ends.
Inputs may be any that keep to these rules, and one draw needn't show every extreme that they name: `targets`: in each row every value 0 to 127 appears exactly once, the rest of the slots are -1 (their populations and flags are unused). No device sends more than 2 blocks to one device of its row, a bound reached in every row; in every row some device holds 9 blocks.
All inputs are finite; a program needn't handle non-finite values. No bound on the sum of `flags` on one device may be relied on, other than what follows from the above.
Results may differ from the reference program's by a relative error of at most 0.0003.
Values sent between devices are 32-bit elements; how exact they have to be, the bound alone decides.
No kernel may reach another device: no remote copies, remote signals or barrier semaphores. Data moves between devices by JAX's collectives and lax.ppermute only.
A program may use at most 192 MiB of HBM per device.

```python
import math
import jax
import jax.numpy as jnp
import numpy as np
from jax import lax

BS = 16
BZ = 8
STEPS = 1
OLD_CAP = 9
CELLS = 4096
N_GX = 16
N_GY = 8


def migration_row(key):
    key_label, key_depth, key_slot = jax.random.split(key, 3)
    blocks = jnp.arange(N_GX * BZ, dtype=jnp.int32)
    receiver = blocks // BZ
    level = blocks % BZ
    sender = (receiver + level) % N_GX
    moved = (sender % 2 == 1) & (level >= 1) & (level <= OLD_CAP - BZ)
    sender = jnp.where(moved, sender - 1, sender)
    relabel = jax.random.permutation(key_label, N_GX).astype(jnp.int32)
    sender = relabel[sender]
    depth_order = jax.vmap(lambda k: jax.random.permutation(k, BZ))(jax.random.split(key_depth, N_GX)).astype(jnp.int32)
    value = receiver * BZ + depth_order[receiver, level]
    earlier = (sender[None, :] == sender[:, None]) & (blocks[None, :] < blocks[:, None])
    rank = jnp.sum(earlier.astype(jnp.int32), axis=1)
    slot_order = jax.vmap(lambda k: jax.random.permutation(k, OLD_CAP))(jax.random.split(key_slot, N_GX)).astype(jnp.int32)
    slot = slot_order[sender, rank]
    empty = jnp.full((N_GX * OLD_CAP,), -1, dtype=jnp.int32)
    return empty.at[sender * OLD_CAP + slot].set(value)


def draw_targets(key, part):
    key = jax.random.fold_in(key, 11)
    return jax.vmap(migration_row)(jax.random.split(key, N_GY))


def set_ends(values, rng, smallest, high):
    longest = values.shape.index(max(values.shape))
    spots = []
    for shift in (0, 1):
        where = [jax.random.randint(jax.random.fold_in(rng, axis), (), 0, length) for axis, length in enumerate(values.shape)]
        where[longest] = (where[longest] + shift) % values.shape[longest]
        spots.append(tuple(where))
    return values.at[spots[0]].set(smallest).at[spots[1]].set(high)


def shard_levels(rng, dims, pieces, smallest, top_value):
    gain, own = 1.0, jax.random.fold_in(rng, 6)
    for dim, shards_of in pieces:
        heights = jnp.exp(jax.random.uniform(jax.random.fold_in(own, dim), (shards_of,), jnp.float32, smallest / len(pieces), top_value / len(pieces)))
        gain = gain * jnp.repeat(heights, dims[dim] // shards_of).reshape([-1 if axis == dim else 1 for axis in range(len(dims))])
    return gain


def gaussian(rng, shape, scale, limit, cuts=(), kind=jnp.bfloat16):
    drawn = jax.random.normal(rng, shape, jnp.float32) * scale
    if len(cuts) > 0:
        drawn = shard_levels(rng, shape, cuts, -0.22, 0.18) * drawn
    return jnp.clip(drawn, min=-limit, max=limit).astype(kind)


def setup_inputs(seed: int = 0) -> dict:
    arg_keys = jax.random.split(jax.random.key(seed), 6)
    return {
        "hydro_old": gaussian(arg_keys[0], (N_GY, N_GX * OLD_CAP, 27, CELLS), 0.1, 0.8, ((0, 8), (1, 16)), jnp.float32),
        "phase_old": gaussian(arg_keys[1], (N_GY, N_GX * OLD_CAP, 15, CELLS), 0.1, 0.8, ((0, 8), (1, 16)), jnp.float32),
        "targets": draw_targets(jax.random.fold_in(arg_keys[5], 71), 0),
        "flags": set_ends((jax.random.randint(arg_keys[3], (N_GY, N_GX * OLD_CAP), 0, 2) < 1).astype(jnp.int32), jax.random.fold_in(arg_keys[3], 1), 0, 1),
        "relax_rates": jnp.clip(jnp.exp(jax.random.uniform(arg_keys[4], (27,), jnp.float32, math.log(0.8), math.log(1.8))), 0.8, 1.8),
    }


def lattice_tables():
    full_list = [[a, b, c] for a in (-1, 0, 1) for b in (-1, 0, 1) for c in (-1, 0, 1)]
    level = [abs(row[0]) + abs(row[1]) + abs(row[2]) for row in full_list]
    full_table = [8.0 / 27.0, 2.0 / 27.0, 1.0 / 54.0, 1.0 / 216.0]
    small_table = [2.0 / 9.0, 1.0 / 9.0, 0.0, 1.0 / 72.0]
    full = np.array(full_list, dtype=np.float32)
    full_weight = np.array([full_table[v] for v in level], dtype=np.float32)
    small = np.array([row for row, v in zip(full_list, level) if v != 2], dtype=np.float32)
    small_weight = np.array([small_table[v] for v in level if v != 2], dtype=np.float32)
    single = np.array([[1.0, 1.0, 1.0], [-1.0, 0.0, 1.0], [1.0, 0.0, 1.0]], dtype=np.float32)
    single_inverse = np.array([[0.0, -0.5, 0.5], [1.0, 0.0, -1.0], [0.0, 0.5, 0.5]], dtype=np.float32)
    moment = np.kron(np.kron(single, single), single)
    inverse = np.kron(np.kron(single_inverse, single_inverse), single_inverse)
    shear_mask = np.zeros(27, dtype=np.float32)
    shear_mask[[4, 10, 12]] = 1.0
    return (full, full_weight, small, small_weight, moment, inverse, shear_mask)

def expand(table, ndim):
    return jnp.asarray(table).reshape((table.shape[0],) + (1,) * (ndim - 1))

def fluid_velocity(hydro):
    full = lattice_tables()[0]
    return jnp.einsum('qc,q...->c...', jnp.asarray(full), hydro, precision=lax.Precision.HIGHEST)

def collide_hydro(hydro, phase, relax_rates):
    full, full_weight, small, small_weight, moment, inverse, shear_mask = lattice_tables()
    ndim = hydro.ndim
    pressure = lax.optimization_barrier(jnp.sum(hydro, axis=0))
    velocity = fluid_velocity(hydro)
    along = jnp.einsum('qc,c...->q...', jnp.asarray(full), velocity, precision=lax.Precision.HIGHEST)
    speed = lax.optimization_barrier(jnp.sum(velocity * velocity, axis=0))
    equil = expand(full_weight, ndim) * (pressure + 3.0 * along + 4.5 * along * along - 1.5 * speed)
    clipped = jnp.clip(phase, 0.0, 1.0)
    density = 0.001 + 0.999 * clipped
    dynamic = 1e-05 + 0.09999 * clipped
    shear_rate = 1.0 / (0.5 + 3.0 * dynamic / density)
    mask = expand(shear_mask, ndim)
    rates = relax_rates.reshape((27,) + (1,) * (ndim - 1)) * (1.0 - mask) + mask * shear_rate[None]
    spatial = hydro.shape[1:]
    moments = jnp.dot(jnp.asarray(moment), (hydro - equil).reshape(27, -1), precision=lax.Precision.HIGHEST)
    scaled = rates * moments.reshape((27,) + spatial)
    back = jnp.dot(jnp.asarray(inverse), scaled.reshape(27, -1), precision=lax.Precision.HIGHEST)
    return hydro - back.reshape(hydro.shape)

def collide_phase(phase_pop, phase, grad, velocity, flag_field):
    small, small_weight = lattice_tables()[2:4]
    ndim = phase_pop.ndim
    length = jnp.sqrt(lax.optimization_barrier(jnp.sum(grad * grad, axis=0)) + 0.25)
    normal = grad / length[None]
    along = jnp.einsum('kc,c...->k...', jnp.asarray(small), velocity, precision=lax.Precision.HIGHEST)
    facing = jnp.einsum('kc,c...->k...', jnp.asarray(small), normal, precision=lax.Precision.HIGHEST)
    weight = expand(small_weight, ndim)
    equil = weight * phase * (1.0 + 3.0 * along) + flag_field * weight * 4.0 * phase * (1.0 - phase) * facing
    return phase_pop - (phase_pop - equil) / 0.7

def phase_gradient(fetch):
    full, full_weight = lattice_tables()[:2]
    parts = [None, None, None]
    for index in range(27):
        offset = [int(v) for v in full[index]]
        if offset == [0, 0, 0]:
            continue
        term = float(3.0 * full_weight[index]) * fetch(offset[0], offset[1], offset[2])
        for axis_index in range(3):
            if offset[axis_index] != 0:
                piece = term if offset[axis_index] > 0 else -term
                parts[axis_index] = piece if parts[axis_index] is None else parts[axis_index] + piece
    return jnp.stack(parts)

def place_field(blocks, comps):
    shaped = blocks.reshape(N_GY, N_GX, BZ, comps, BS, BS, BS)
    return shaped.transpose(3, 1, 4, 0, 5, 2, 6).reshape(comps, N_GX * BS, N_GY * BS, BZ * BS)

def reference(hydro_old, phase_old, targets, flags, relax_rates):
    full, full_weight, small = lattice_tables()[:3]
    values = jnp.arange(N_GX * BZ, dtype=jnp.int32)
    match = targets[:, None, :] == values[None, :, None]
    where_from = jnp.argmax(match, axis=2).astype(jnp.int32)
    row_index = jnp.arange(N_GY, dtype=jnp.int32)[:, None]
    hydro = place_field(hydro_old[row_index, where_from], 27)
    phase_pop = place_field(phase_old[row_index, where_from], 15)
    flag_blocks = jnp.take_along_axis(flags, where_from, axis=1).reshape(N_GY, N_GX, BZ).transpose(1, 0, 2)
    flag_field = jnp.repeat(jnp.repeat(jnp.repeat(flag_blocks, BS, axis=0), BS, axis=1), BS, axis=2).astype(jnp.float32)
    for turn_index in range(STEPS):
        phase = lax.optimization_barrier(jnp.sum(phase_pop, axis=0))
        grad = phase_gradient(lambda a, b, c: jnp.roll(phase, (-a, -b, -c), axis=(0, 1, 2)))
        velocity = fluid_velocity(hydro)
        hydro_post = collide_hydro(hydro, phase, relax_rates)
        phase_post = collide_phase(phase_pop, phase, grad, velocity, flag_field)
        hydro = jnp.stack([jnp.roll(hydro_post[index], tuple((int(v) for v in full[index])), axis=(0, 1, 2)) for index in range(27)])
        phase_pop = jnp.stack([jnp.roll(phase_post[index], tuple((int(v) for v in small[index])), axis=(0, 1, 2)) for index in range(15)])
    return (hydro, phase_pop)
```

```python
import functools

import jax
import jax.numpy as jnp
import numpy as np
from jax import lax
from jax.experimental import pallas as pl
from jax.experimental.pallas import tpu as pltpu
from jax.sharding import PartitionSpec as P

BS = 16
BZ = 8
SLOT_ROWS = 88
LANES = 128
VMEM_LIMIT = 56 * 1024 * 1024

FULL = [(a, b, c) for a in (-1, 0, 1) for b in (-1, 0, 1) for c in (-1, 0, 1)]
SMALL = [v for v in FULL if sum(map(abs, v)) != 2]
ORDER = sorted(
    [("h", q, v) for q, v in enumerate(FULL)] + [("p", k, v) for k, v in enumerate(SMALL)],
    key=lambda t: (t[2][0], t[2][1], t[0], t[1]),
)
PLACE = {(kind, index): n for n, (kind, index, _) in enumerate(ORDER)}
UP_FACE = [n for n, t in enumerate(ORDER) if t[2][1] == 1]
DOWN_FACE = [n for n, t in enumerate(ORDER) if t[2][1] == -1]


def runs(places):
    out = []
    for n in places:
        if out and out[-1][1] == n:
            out[-1][1] = n + 1
        else:
            out.append([n, n + 1])
    return out


def pack_kernel(place_ref, h_ref, p_ref, target_ref, flag_ref, out_ref, here_ref):
    step = pl.program_id(0)
    slots = target_ref.shape[1]

    here_ref[0] = place_ref[0]

    @pl.when(step < slots)
    def _():
        for part in range(4):
            rows = pl.ds(part * 8, 8)
            groups = [[h_ref[0, 4 * n + m, rows, :] for m in range(4)] for n in range(6)]
            groups += [[p_ref[0, 4 * n + m, rows, :] for m in range(4)] for n in range(3)]
            last_h = [h_ref[0, 24 + m, rows, :] for m in range(3)]
            last_p = [p_ref[0, 12 + m, rows, :] for m in range(3)]
            groups += [last_p + [beside(p_ref, part, -1)], last_h + [beside(p_ref, part, 1)]]
            for n, group in enumerate(groups):
                for m, value in enumerate(swap_bits(group, 0, 2)):
                    out_ref[part * 4 + m, pl.ds(n * 8, 8), :] = value

    @pl.when(step == slots)
    def _():
        for i in range(BS):
            out_ref[i, 0:1, 0:slots] = target_ref[...].astype(jnp.float32)
            out_ref[i, 1:2, 0:slots] = flag_ref[...].astype(jnp.float32)


def beside(p_ref, part, side):
    near = sum(p_ref[0, k, pl.ds(part * 8, 8), :] for k in range(15))
    other = (part + side) % 4
    far = sum(p_ref[0, k, pl.ds(other * 8, 8), :] for k in range(15))
    row = lax.broadcasted_iota(jnp.int32, (8, LANES), 0)
    if side < 0:
        return jnp.where(row < 2, pltpu.roll(far, 2, 0), pltpu.roll(near, 2, 0))
    return jnp.where(row >= 6, pltpu.roll(far, 6, 0), pltpu.roll(near, 6, 0))


def pack(place, hydro, phase, targets, flags):
    slots = hydro.shape[0]
    whole = pl.BlockSpec(memory_space=pltpu.VMEM)
    return pl.pallas_call(
        pack_kernel,
        grid=(slots + 1,),
        in_specs=[
            pl.BlockSpec(memory_space=pltpu.SMEM),
            pl.BlockSpec((1, 27, 32, LANES), lambda s: (jnp.minimum(s, slots - 1), 0, 0, 0)),
            pl.BlockSpec((1, 15, 32, LANES), lambda s: (jnp.minimum(s, slots - 1), 0, 0, 0)),
            whole,
            whole,
        ],
        out_specs=[
            pl.BlockSpec((BS, SLOT_ROWS, LANES), lambda s: (0, s, 0)),
            pl.BlockSpec(memory_space=pltpu.SMEM),
        ],
        out_shape=[
            jax.ShapeDtypeStruct((BS, slots * SLOT_ROWS + 8, LANES), jnp.float32),
            jax.ShapeDtypeStruct((1,), jnp.int32),
        ],
        compiler_params=pltpu.CompilerParams(vmem_limit_bytes=VMEM_LIMIT),
    )(place, hydro.reshape(slots, 27, 32, LANES), phase.reshape(slots, 15, 32, LANES), targets, flags)


def swap_bits(values, axis, unit):
    count = len(values)
    size = count * unit
    position = lax.broadcasted_iota(jnp.int32, (8, LANES), axis) // unit
    step = 1
    while step < count:
        high = (position & step) != 0
        fresh = list(values)
        for n in range(count):
            if n & step:
                continue
            a, b = values[n], values[n + step]
            fresh[n] = jnp.where(high, pltpu.roll(b, step * unit, axis), a)
            fresh[n + step] = jnp.where(high, b, pltpu.roll(a, size - step * unit, axis))
        values = fresh
        step *= 2
    return values


GROUPS = [[4 * n + m for m in range(4)] for n in range(6)]
GROUPS += [[27 + 4 * n + m for m in range(4)] for n in range(3)]
GROUPS += [[39, 40, 41, 42], [24, 25, 26, 43]]


def spread_kernel(where_ref, *refs):
    blocks, out_ref = refs[:8], refs[8]
    for group in range(SLOT_ROWS // 8):
        values = [blocks[level][0, pl.ds(group * 8, 8), :] for level in range(8)]
        values = swap_bits(values, 1, 16)
        values = swap_bits(values, 0, 1)
        for n in range(8):
            out_ref[0, GROUPS[group][n // 2], pl.ds((n % 2) * 8, 8), :] = values[n]
    total = out_ref[0, 27]
    for k in range(1, 15):
        total = total + out_ref[0, 27 + k]
    out_ref[0, 44] = total


def spread(where, got):
    def block(level):
        return pl.BlockSpec(
            (1, SLOT_ROWS, LANES), lambda d, w: (w[0, d * 8 + level], w[1, d * 8 + level], 0)
        )

    return pl.pallas_call(
        spread_kernel,
        grid_spec=pltpu.PrefetchScalarGridSpec(
            num_scalar_prefetch=1,
            grid=(16,),
            in_specs=[block(level) for level in range(8)],
            out_specs=pl.BlockSpec((1, 45, BS, LANES), lambda d, w: (d, 0, 0, 0)),
        ),
        out_shape=jax.ShapeDtypeStruct((16, 45, BS, LANES), jnp.float32),
        compiler_params=pltpu.CompilerParams(vmem_limit_bytes=VMEM_LIMIT),
    )(where, *([got] * 8))


def to_moments(f):
    f = list(f)
    for stride in (1, 3, 9):
        for n in range(27):
            if (n // stride) % 3 == 0:
                low, mid, high = f[n], f[n + stride], f[n + 2 * stride]
                both = low + high
                f[n], f[n + stride], f[n + 2 * stride] = both + mid, high - low, both
    return f


def from_moments(m):
    m = list(m)
    for stride in (1, 3, 9):
        for n in range(27):
            if (n // stride) % 3 == 0:
                zero, one, two = m[n], m[n + stride], m[n + 2 * stride]
                low, high = two - one, two + one
                m[n], m[n + stride], m[n + 2 * stride] = low, zero - (low + high), high
    return m


def equil_moments(pressure, velocity):
    x, y, z = velocity
    squares = (x * x, y * y, z * z)
    cross = {(1, 1, 0): x * y, (1, 0, 1): x * z, (0, 1, 1): y * z}
    third = pressure * (1.0 / 3.0)
    total = squares[0] + squares[1] + squares[2]
    out = [None] * 27
    for q in range(27):
        powers = (q // 9, q // 3 % 3, q % 3)
        ones = tuple(int(n == 1) for n in powers)
        scale = (1.0 / 3.0) ** sum(n == 2 for n in powers)
        if sum(ones) == 0:
            two = [squares[n] for n in range(3) if powers[n] == 2]
            value = pressure if not two else pressure + 3.0 * sum(two[1:], two[0])
            out[q] = value if scale == 1.0 else scale * value
        elif sum(ones) == 1:
            value = velocity[ones.index(1)]
            out[q] = value if scale == 1.0 else scale * value
        elif sum(ones) == 2:
            out[q] = cross[ones] if scale == 1.0 else scale * cross[ones]
        else:
            out[q] = 0.0
    return out


def weighted(v, table):
    return table[sum(map(abs, v))]


FULL_WEIGHT = [8.0 / 27.0, 2.0 / 27.0, 1.0 / 54.0, 1.0 / 216.0]
SMALL_WEIGHT = [2.0 / 9.0, 1.0 / 9.0, 0.0, 1.0 / 72.0]


def dot(v, parts):
    total = None
    for c, part in zip(v, parts):
        if c != 0:
            if total is None:
                total = part if c > 0 else -part
            else:
                total = total + part if c > 0 else total - part
    return total


def collide_kernel(place_ref, rate_ref, n_ref, before_ref, after_ref, low_ref, high_ref, flag_ref, out_ref):
    d = pl.program_id(0)
    place = place_ref[0]
    left = jnp.where(place == 0, (d + 15) % 16, d)
    right = jnp.where(place == 15, (d + 1) % 16, d)
    row = lax.broadcasted_iota(jnp.int32, (BS, LANES), 0)

    planes = []
    for ref, index, which in ((before_ref, left, 0), (None, d, 2), (after_ref, right, 1)):
        centre = n_ref[0, 44] if ref is None else ref[0, 0]
        low = low_ref[index, pl.ds(which, 1), :]
        high = high_ref[index, pl.ds(which, 1), :]
        minus = jnp.where(row == 0, low, pltpu.roll(centre, 1, 0))
        plus = jnp.where(row == BS - 1, high, pltpu.roll(centre, BS - 1, 0))
        smooth_y = (2.0 / 3.0) * centre + (1.0 / 6.0) * (minus + plus)
        planes.append((smooth_y, plus - minus))

    def along_z(v):
        return pltpu.roll(v, LANES - 1, 1), pltpu.roll(v, 1, 1)

    def smooth_z(v):
        plus, minus = along_z(v)
        return (2.0 / 3.0) * v + (1.0 / 6.0) * (plus + minus)

    grad_x = 0.5 * smooth_z(planes[2][0] - planes[0][0])
    sides = planes[0][1] + planes[2][1]
    grad_y = 0.5 * smooth_z((2.0 / 3.0) * planes[1][1] + (1.0 / 6.0) * sides)
    sides = planes[0][0] + planes[2][0]
    plus, minus = along_z((2.0 / 3.0) * planes[1][0] + (1.0 / 6.0) * sides)
    grad_z = 0.5 * (plus - minus)
    flag_line = flag_ref[pl.ds(d, 1), :]

    for half in range(2):
        rows = slice(half * 8, half * 8 + 8)
        at = pl.ds(half * 8, 8)
        f = [n_ref[0, q, at, :] for q in range(27)]
        phase = n_ref[0, 44, at, :]
        raw = to_moments(f)
        velocity = (raw[9], raw[3], raw[1])
        rest = equil_moments(raw[0], velocity)
        clipped = jnp.clip(phase, 0.0, 1.0)
        density = 0.001 + 0.999 * clipped
        dynamic = 1e-05 + 0.09999 * clipped
        shear = density / (0.5 * density + 3.0 * dynamic)
        scaled = [0.0] * 27
        for q in range(27):
            fold = 0.5 ** sum(n != 0 for n in (q // 9, q // 3 % 3, q % 3))
            rate = shear if q in (4, 10, 12) else rate_ref[q]
            scaled[q] = (rate * fold) * (raw[q] - rest[q])
        back = from_moments(scaled)

        def put(kind, index, v, value):
            if v[2] != 0:
                value = pltpu.roll(value, v[2] % LANES, 1)
            to = d if v[0] == 0 else (left if v[0] < 0 else right)
            out_ref[to, PLACE[kind, index], at, :] = value

        for q in range(27):
            put("h", q, FULL[q], f[q] - back[q])

        g = (grad_x[rows], grad_y[rows], grad_z[rows])
        scale = lax.rsqrt(g[0] * g[0] + g[1] * g[1] + g[2] * g[2] + 0.25)
        sharp = flag_line * (4.0 * phase * (1.0 - phase)) * scale
        drive = [3.0 * phase * velocity[n] + sharp * g[n] for n in range(3)]
        for k in range(15):
            w = weighted(SMALL[k], SMALL_WEIGHT)
            pop = n_ref[0, 27 + k, at, :]
            push = dot(SMALL[k], drive)
            equil = w * (phase if push is None else phase + push)
            put("p", k, SMALL[k], pop - (pop - equil) * (1.0 / 0.7))


def collide(place, rates, field, low, high, flag_lines):
    whole = pl.BlockSpec(memory_space=pltpu.VMEM)

    def shifted(comp, edge, step):
        return pl.BlockSpec(
            (1, 1, BS, LANES),
            lambda d, i: (jnp.where(i[0] == edge, (d + step) % 16, d), comp, 0, 0),
        )

    return pl.pallas_call(
        collide_kernel,
        grid_spec=pltpu.PrefetchScalarGridSpec(
            num_scalar_prefetch=1,
            grid=(16,),
            in_specs=[
                pl.BlockSpec(memory_space=pltpu.SMEM),
                pl.BlockSpec((1, 45, BS, LANES), lambda d, i: (d, 0, 0, 0)),
                shifted(42, 0, 15),
                shifted(43, 15, 1),
                whole,
                whole,
                whole,
            ],
            out_specs=pl.BlockSpec((16, 42, BS, LANES), lambda d, i: (0, 0, 0, 0)),
        ),
        out_shape=jax.ShapeDtypeStruct((16, 42, BS, LANES), jnp.float32),
        compiler_params=pltpu.CompilerParams(vmem_limit_bytes=VMEM_LIMIT),
    )(place, rates, field, field, field, low, high, flag_lines)


def finish_kernel(minus_ref, zero_ref, plus_ref, low_ref, high_ref, hydro_ref, phase_ref):
    x = pl.program_id(0)
    row = lax.broadcasted_iota(jnp.int32, (BS, LANES), 0)
    for n, (kind, index, v) in enumerate(ORDER):
        source = (minus_ref, zero_ref, plus_ref)[v[0] + 1]
        value = source[0, n % 14]
        at = (x - v[0] + 16) % 16
        if v[1] == 1:
            face = low_ref[at, pl.ds(UP_FACE.index(n), 1), :]
            value = jnp.where(row == 0, face, pltpu.roll(value, 1, 0))
        elif v[1] == -1:
            face = high_ref[at, pl.ds(DOWN_FACE.index(n), 1), :]
            value = jnp.where(row == BS - 1, face, pltpu.roll(value, BS - 1, 0))
        (hydro_ref if kind == "h" else phase_ref)[index, 0] = value


def finish(got, low, high):
    whole = pl.BlockSpec(memory_space=pltpu.VMEM)

    def part(group, step):
        return pl.BlockSpec((1, 14, BS, LANES), lambda x: ((x + step) % 16, group, 0, 0))

    return pl.pallas_call(
        finish_kernel,
        grid=(16,),
        in_specs=[part(0, 1), part(1, 0), part(2, 15), whole, whole],
        out_specs=[
            pl.BlockSpec((27, 1, BS, LANES), lambda x: (0, x, 0, 0)),
            pl.BlockSpec((15, 1, BS, LANES), lambda x: (0, x, 0, 0)),
        ],
        out_shape=[
            jax.ShapeDtypeStruct((27, BS, BS, LANES), jnp.float32),
            jax.ShapeDtypeStruct((15, BS, BS, LANES), jnp.float32),
        ],
        compiler_params=pltpu.CompilerParams(vmem_limit_bytes=VMEM_LIMIT),
    )(got, got, got, low, high)


def swap_faces(upper, lower):
    size = lax.axis_size("gy")
    up = [(i, (i + 1) % size) for i in range(size)]
    down = [(j, i) for i, j in up]
    return lax.ppermute(upper, "gy", up), lax.ppermute(lower, "gy", down)


def on_device(hydro_old, phase_old, targets, flags, relax_rates):
    place = lax.axis_index("gx").astype(jnp.int32).reshape(1)
    slots = targets.shape[1]
    packed, place = pack(place, hydro_old[0], phase_old[0], targets, flags)
    got = lax.all_to_all(packed, "gx", split_axis=0, concat_axis=0, tiled=True)
    label = got[:, slots * SLOT_ROWS, :slots].astype(jnp.int32)
    flag = got[:, slots * SLOT_ROWS + 1, :slots]
    match = label.reshape(1, -1) == jnp.arange(128, dtype=jnp.int32)[:, None]
    order = jnp.arange(16 * slots, dtype=jnp.int32)
    where = jnp.sum(jnp.where(match, order[None, :], 0), axis=1)
    where = jnp.stack([where // slots, where % slots])
    flag_of = jnp.sum(jnp.where(match, flag.reshape(1, -1), 0.0), axis=1)
    flag_lines = jnp.repeat(flag_of.reshape(16, BZ), BS, axis=1)

    field = spread(where, got)
    low, high = swap_faces(field[:, 42:45, BS - 1, :], field[:, 42:45, 0, :])
    send = collide(place, relax_rates, field, low, high, flag_lines)
    final = lax.all_to_all(send, "gx", split_axis=0, concat_axis=0, tiled=True)
    upper = jnp.concatenate([final[:, a:b, BS - 1, :] for a, b in runs(UP_FACE)], axis=1)
    lower = jnp.concatenate([final[:, a:b, 0, :] for a, b in runs(DOWN_FACE)], axis=1)
    low, high = swap_faces(upper, lower)
    return tuple(finish(final, low, high))


def solution(mesh):
    in_specs = (
        P("gy", "gx", None, None),
        P("gy", "gx", None, None),
        P("gy", "gx"),
        P("gy", "gx"),
        P(),
    )
    out_specs = (P(None, "gx", "gy", None), P(None, "gx", "gy", None))
    return jax.shard_map(
        on_device, mesh=mesh, in_specs=in_specs, out_specs=out_specs, check_vma=False
    )
```

```python
import functools

import jax
import jax.numpy as jnp
import numpy as np
from jax import lax
from jax.experimental import pallas as pl
from jax.experimental.pallas import tpu as pltpu
from jax.sharding import PartitionSpec as P

BS = 16
BZ = 8
SLOT_ROWS = 88
AHEAD = 4
LANES = 128
MIB = 1024 * 1024
ANY = pl.BlockSpec(memory_space=pl.ANY)
SMEM = pl.BlockSpec(memory_space=pltpu.SMEM)
WHOLE = pl.BlockSpec(memory_space=pltpu.VMEM)


def room(mib):
    return pltpu.CompilerParams(vmem_limit_bytes=mib * MIB)


def buffer(*shape):
    return pltpu.VMEM(shape, jnp.float32)


def made(*shape):
    return jax.ShapeDtypeStruct(shape, jnp.float32)

FULL = [(a, b, c) for a in (-1, 0, 1) for b in (-1, 0, 1) for c in (-1, 0, 1)]
SMALL = [v for v in FULL if sum(map(abs, v)) != 2]
ORDER = sorted(
    [("h", q, v) for q, v in enumerate(FULL)] + [("p", k, v) for k, v in enumerate(SMALL)],
    key=lambda t: (t[2][0], t[0], t[2][1] if t[0] == "h" else -t[2][1], t[1]),
)
PLACE = {(kind, index): n for n, (kind, index, _) in enumerate(ORDER)}
UP_FACE = [n for n, t in enumerate(ORDER) if t[2][1] == 1]
DOWN_FACE = [n for n, t in enumerate(ORDER) if t[2][1] == -1]


def runs(places):
    out = []
    for n in places:
        if out and out[-1][1] == n:
            out[-1][1] = n + 1
        else:
            out.append([n, n + 1])
    return out


def pack_kernel(
    place_ref, h_in, p_in, target_ref, flag_ref, out, here_ref, h_ref, p_ref, o_ref, tag_ref, h_sem, p_sem, o_sem, tag_sem
):
    slots = target_ref.shape[1]
    here_ref[0] = place_ref[0]

    def load(s):
        return (
            pltpu.make_async_copy(h_in.at[s], h_ref.at[s], h_sem.at[s]),
            pltpu.make_async_copy(p_in.at[s], p_ref.at[s], p_sem.at[s]),
        )

    def leave(s):
        rows = pl.ds(pl.multiple_of(s * SLOT_ROWS, 8), SLOT_ROWS)
        return pltpu.make_async_copy(o_ref.at[s], out.at[:, rows, :], o_sem.at[s])

    for s in range(slots):
        for copy in load(s):
            copy.start()
    tag_ref[:, 0:1, 0:slots] = jnp.broadcast_to(target_ref[...].astype(jnp.float32), (BS, 1, slots))
    tag_ref[:, 1:2, 0:slots] = jnp.broadcast_to(flag_ref[...].astype(jnp.float32), (BS, 1, slots))
    tags = pltpu.make_async_copy(tag_ref, out.at[:, pl.ds(slots * SLOT_ROWS, 8), :], tag_sem)
    tags.start()

    @pl.loop(0, slots)
    def _(s):
        for copy in load(s):
            copy.wait()
        totals = [sum(p_ref[s, k, pl.ds(part * 8, 8), :] for k in range(15)) for part in range(4)]
        for part in range(4):
            rows = pl.ds(part * 8, 8)
            groups = [[h_ref[s, 4 * n + m, rows, :] for m in range(4)] for n in range(6)]
            groups += [[p_ref[s, 4 * n + m, rows, :] for m in range(4)] for n in range(3)]
            last_h = [h_ref[s, 24 + m, rows, :] for m in range(3)]
            last_p = [p_ref[s, 12 + m, rows, :] for m in range(3)]
            groups += [last_p + [beside(totals, part, -1)], last_h + [beside(totals, part, 1)]]
            for n, group in enumerate(groups):
                for m, value in enumerate(swap_bits(group, 0, 2)):
                    o_ref[s, part * 4 + m, pl.ds(n * 8, 8), :] = value
        leave(s).start()

    for s in range(slots):
        leave(s).wait()
    tags.wait()


def beside(totals, part, side):
    near, far = totals[part], totals[(part + side) % 4]
    row = lax.broadcasted_iota(jnp.int32, (8, LANES), 0)
    if side < 0:
        return jnp.where(row < 2, pltpu.roll(far, 2, 0), pltpu.roll(near, 2, 0))
    return jnp.where(row >= 6, pltpu.roll(far, 6, 0), pltpu.roll(near, 6, 0))


def pack(place, hydro, phase, targets, flags):
    slots = hydro.shape[0]
    return pl.pallas_call(
        pack_kernel,
        in_specs=[SMEM, ANY, ANY, WHOLE, WHOLE],
        out_specs=[ANY, SMEM],
        out_shape=[
            made(BS, slots * SLOT_ROWS + 8, LANES),
            jax.ShapeDtypeStruct((1,), jnp.int32),
        ],
        scratch_shapes=[
            buffer(slots, 27, 32, LANES),
            buffer(slots, 15, 32, LANES),
            buffer(slots, BS, SLOT_ROWS, LANES),
            buffer(BS, 8, LANES),
            pltpu.SemaphoreType.DMA((slots,)),
            pltpu.SemaphoreType.DMA((slots,)),
            pltpu.SemaphoreType.DMA((slots,)),
            pltpu.SemaphoreType.DMA,
        ],
        compiler_params=room(60),
    )(place, hydro.reshape(slots, 27, 32, LANES), phase.reshape(slots, 15, 32, LANES), targets, flags)


def swap_bits(values, axis, unit):
    count = len(values)
    size = count * unit
    position = lax.broadcasted_iota(jnp.int32, (8, LANES), axis) // unit
    step = 1
    while step < count:
        high = (position & step) != 0
        fresh = list(values)
        for n in range(count):
            if n & step:
                continue
            a, b = values[n], values[n + step]
            fresh[n] = jnp.where(high, pltpu.roll(b, step * unit, axis), a)
            fresh[n + step] = jnp.where(high, b, pltpu.roll(a, size - step * unit, axis))
        values = fresh
        step *= 2
    return values


def swap_lanes(values):
    position = lax.broadcasted_iota(jnp.int32, (8, LANES), 1) // 16

    def skew(parts):
        for step in (1, 2, 4):
            high = (position & step) != 0
            parts = [jnp.where(high, parts[(n - step) % 8], parts[n]) for n in range(8)]
        return parts

    parts = skew([values[-n % 8] for n in range(8)])
    return skew([parts[0]] + [pltpu.roll(parts[n], LANES - 16 * n, 1) for n in range(1, 8)])


GROUPS = [[4 * n + m for m in range(4)] for n in range(6)]
GROUPS += [[27 + 4 * n + m for m in range(4)] for n in range(3)]
GROUPS += [[39, 40, 41, 42], [24, 25, 26, 43]]


def survey_kernel(got, code_ref, sum_ref, up_ref, down_ref, tag_ref, b_ref, code_s, tag_sem, b_sem, code_sem):
    slots = b_ref.shape[0]
    tags = pltpu.make_async_copy(got.at[:, pl.ds(slots * SLOT_ROWS, 8), :], tag_ref, tag_sem)
    tags.start()
    loads = [
        pltpu.make_async_copy(got.at[:, pl.ds(t * SLOT_ROWS + 48, 40), :], b_ref.at[t], b_sem.at[t])
        for t in range(slots)
    ]
    for copy in loads:
        copy.start()
    tags.wait()

    row = lax.broadcasted_iota(jnp.int32, (8, LANES), 0)
    value = lax.broadcasted_iota(jnp.int32, (8, LANES), 1).astype(jnp.float32)
    code = jnp.zeros((8, LANES), jnp.float32)
    for half in range(2):
        label = tag_ref[pl.ds(half * 8, 8), 0, :]
        flag = tag_ref[pl.ds(half * 8, 8), 1, :]
        sender = ((row + half * 8) * 32).astype(jnp.float32)
        for t in range(slots):
            match = jnp.broadcast_to(label[:, t : t + 1], (8, LANES)) == value
            entry = sender + (2.0 * t + jnp.broadcast_to(flag[:, t : t + 1], (8, LANES)))
            code = code + jnp.where(match, entry, 0.0)
    code_ref[...] = jnp.sum(code, axis=0, keepdims=True).astype(jnp.int32)
    table = pltpu.make_async_copy(code_ref, code_s, code_sem)
    table.start()
    table.wait()
    for copy in loads:
        copy.wait()

    @pl.loop(0, 16)
    def _(d):
        values = []
        for level in range(8):
            sender, slot, _ = decode(code_s[0, d * 8 + level])
            parts = [b_ref[slot, sender, pl.ds(n * 8, 8), :] for n in range(5)]
            own = parts[0] + parts[1] + parts[2] + jnp.where(row < 6, parts[3], 0.0)
            own = own + pltpu.roll(own, 2, 0)
            own = own + pltpu.roll(own, 4, 0)
            beyond = jnp.where(row < 4, pltpu.roll(parts[4], 4, 0), own)
            values.append(jnp.where(row < 2, pltpu.roll(parts[3], 2, 0), beyond))
        values = swap_bits(swap_lanes(values), 0, 1)
        for n in range(6):
            sum_ref[d, n // 2, pl.ds((n % 2) * 8, 8), :] = values[n]
        up_ref[d] = sum_ref[d, :, BS - 1, :]
        down_ref[d] = sum_ref[d, :, 0, :]


def decode(code):
    return lax.shift_right_logical(code, 5), lax.shift_right_logical(code, 1) & 15, code & 1


def survey(got, slots):
    return pl.pallas_call(
        survey_kernel,
        in_specs=[ANY],
        out_specs=[WHOLE, WHOLE, WHOLE, WHOLE],
        out_shape=[
            jax.ShapeDtypeStruct((1, LANES), jnp.int32),
            made(16, 3, BS, LANES),
            made(16, 3, LANES),
            made(16, 3, LANES),
        ],
        scratch_shapes=[
            buffer(16, 8, LANES),
            buffer(slots, 16, 40, LANES),
            pltpu.SMEM((1, LANES), jnp.int32),
            pltpu.SemaphoreType.DMA,
            pltpu.SemaphoreType.DMA((slots,)),
            pltpu.SemaphoreType.DMA,
        ],
        compiler_params=room(60),
    )(got)


def to_moments(f):
    f = list(f)
    for stride in (1, 3, 9):
        for n in range(27):
            if (n // stride) % 3 == 0:
                low, mid, high = f[n], f[n + stride], f[n + 2 * stride]
                both = low + high
                f[n], f[n + stride], f[n + 2 * stride] = both + mid, high - low, both
    return f


def from_moments(m):
    m = list(m)
    for stride in (1, 3, 9):
        for n in range(27):
            if (n // stride) % 3 == 0:
                zero, one, two = m[n], m[n + stride], m[n + 2 * stride]
                low, high = two - one, two + one
                m[n], m[n + stride], m[n + 2 * stride] = low, zero - (low + high), high
    return m


def equil_moments(pressure, velocity):
    x, y, z = velocity
    squares = (x * x, y * y, z * z)
    cross = {(1, 1, 0): x * y, (1, 0, 1): x * z, (0, 1, 1): y * z}
    third = pressure * (1.0 / 3.0)
    total = squares[0] + squares[1] + squares[2]
    out = [None] * 27
    for q in range(27):
        powers = (q // 9, q // 3 % 3, q % 3)
        ones = tuple(int(n == 1) for n in powers)
        scale = (1.0 / 3.0) ** sum(n == 2 for n in powers)
        if sum(ones) == 0:
            two = [squares[n] for n in range(3) if powers[n] == 2]
            value = pressure if not two else pressure + 3.0 * sum(two[1:], two[0])
            out[q] = value if scale == 1.0 else scale * value
        elif sum(ones) == 1:
            value = velocity[ones.index(1)]
            out[q] = value if scale == 1.0 else scale * value
        elif sum(ones) == 2:
            out[q] = cross[ones] if scale == 1.0 else scale * cross[ones]
        else:
            out[q] = 0.0
    return out


def weighted(v, table):
    return table[sum(map(abs, v))]


FULL_WEIGHT = [8.0 / 27.0, 2.0 / 27.0, 1.0 / 54.0, 1.0 / 216.0]
SMALL_WEIGHT = [2.0 / 9.0, 1.0 / 9.0, 0.0, 1.0 / 72.0]


def dot(v, parts):
    total = None
    for c, part in zip(v, parts):
        if c != 0:
            if total is None:
                total = part if c > 0 else -part
            else:
                total = total + part if c > 0 else total - part
    return total


def collide_kernel(
    place_ref, rate_ref, code_ref, got, sums, low, high, out,
    sum_ref, low_ref, high_ref, b_ref, n_ref, o_ref, side_sem, b_sem, o_sem,
):
    place = place_ref[0]
    sides = [
        pltpu.make_async_copy(a, b, side_sem.at[n])
        for n, (a, b) in enumerate(((sums, sum_ref), (low, low_ref), (high, high_ref)))
    ]

    def start(d):
        for level in range(8):
            sender, slot, _ = decode(code_ref[0, d * 8 + level])
            rows = pl.ds(pl.multiple_of(slot * SLOT_ROWS, 8), SLOT_ROWS)
            pltpu.make_async_copy(got.at[sender, rows, :], b_ref.at[d, level], b_sem.at[d]).start()

    def leave(d):
        left = jnp.where(place == 0, (d + 15) % 16, d)
        right = jnp.where(place == 15, (d + 1) % 16, d)
        for group, to in enumerate((left, d, right)):
            comps = pl.ds(group * 14, 14)
            yield pltpu.make_async_copy(o_ref.at[d, comps], out.at[to, comps], o_sem.at[d, group])

    for copy in sides:
        copy.start()
    for d in range(AHEAD):
        start(d)
    for copy in sides:
        copy.wait()

    @pl.loop(0, 16)
    def _(d):
        @pl.when(d + AHEAD < 16)
        def _():
            start(d + AHEAD)

        pltpu.make_async_copy(b_ref.at[d], b_ref.at[d], b_sem.at[d]).wait()
        for group, comps in enumerate(GROUPS):
            values = [b_ref[d, level, pl.ds(group * 8, 8), :] for level in range(8)]
            values = swap_bits(swap_lanes(values), 0, 1)
            for n in range(8):
                if comps[n // 2] < 42:
                    n_ref[comps[n // 2], pl.ds((n % 2) * 8, 8), :] = values[n]
        position = lax.broadcasted_iota(jnp.int32, (8, LANES), 1) // 16
        flag_line = jnp.zeros((8, LANES), jnp.float32)
        for level in range(8):
            flag = decode(code_ref[0, d * 8 + level])[2].astype(jnp.float32)
            flag_line = jnp.where(position == level, flag, flag_line)
        collide_plane(d, place, rate_ref, n_ref, sum_ref, low_ref, high_ref, flag_line, o_ref)
        for copy in leave(d):
            copy.start()

    for d in range(16):
        for copy in leave(d):
            copy.wait()


def collide_plane(d, place, rate_ref, n_ref, sum_ref, low_ref, high_ref, flag_line, out_ref):
    left = jnp.where(place == 0, (d + 15) % 16, d)
    right = jnp.where(place == 15, (d + 1) % 16, d)
    row = lax.broadcasted_iota(jnp.int32, (BS, LANES), 0)

    planes = []
    for index, which in ((left, 0), (d, 2), (right, 1)):
        centre = sum_ref[index, which]
        low = low_ref[index, pl.ds(which, 1), :]
        high = high_ref[index, pl.ds(which, 1), :]
        minus = jnp.where(row == 0, low, pltpu.roll(centre, 1, 0))
        plus = jnp.where(row == BS - 1, high, pltpu.roll(centre, BS - 1, 0))
        smooth_y = (2.0 / 3.0) * centre + (1.0 / 6.0) * (minus + plus)
        planes.append((smooth_y, plus - minus))

    def along_z(v):
        return pltpu.roll(v, LANES - 1, 1), pltpu.roll(v, 1, 1)

    def smooth_z(v):
        plus, minus = along_z(v)
        return (2.0 / 3.0) * v + (1.0 / 6.0) * (plus + minus)

    grad_x = 0.5 * smooth_z(planes[2][0] - planes[0][0])
    sides = planes[0][1] + planes[2][1]
    grad_y = 0.5 * smooth_z((2.0 / 3.0) * planes[1][1] + (1.0 / 6.0) * sides)
    sides = planes[0][0] + planes[2][0]
    plus, minus = along_z((2.0 / 3.0) * planes[1][0] + (1.0 / 6.0) * sides)
    grad_z = 0.5 * (plus - minus)

    for half in range(2):
        rows = slice(half * 8, half * 8 + 8)
        at = pl.ds(half * 8, 8)
        f = [n_ref[q, at, :] for q in range(27)]
        phase = sum_ref[d, 2, at, :]
        raw = to_moments(f)
        velocity = (raw[9], raw[3], raw[1])
        rest = equil_moments(raw[0], velocity)
        clipped = jnp.clip(phase, 0.0, 1.0)
        density = 0.001 + 0.999 * clipped
        dynamic = 1e-05 + 0.09999 * clipped
        shear = density / (0.5 * density + 3.0 * dynamic)
        scaled = [0.0] * 27
        for q in range(27):
            fold = 0.5 ** sum(n != 0 for n in (q // 9, q // 3 % 3, q % 3))
            rate = shear if q in (4, 10, 12) else rate_ref[q]
            scaled[q] = (rate * fold) * (raw[q] - rest[q])
        back = from_moments(scaled)

        def put(kind, index, v, value):
            if v[2] != 0:
                value = pltpu.roll(value, v[2] % LANES, 1)
            out_ref[d, PLACE[kind, index], at, :] = value

        for q in range(27):
            put("h", q, FULL[q], f[q] - back[q])

        g = (grad_x[rows], grad_y[rows], grad_z[rows])
        scale = lax.rsqrt(g[0] * g[0] + g[1] * g[1] + g[2] * g[2] + 0.25)
        sharp = flag_line * (4.0 * phase * (1.0 - phase)) * scale
        drive = [3.0 * phase * velocity[n] + sharp * g[n] for n in range(3)]
        for k in range(15):
            w = weighted(SMALL[k], SMALL_WEIGHT)
            pop = n_ref[27 + k, at, :]
            push = dot(SMALL[k], drive)
            equil = w * (phase if push is None else phase + push)
            put("p", k, SMALL[k], pop - (pop - equil) * (1.0 / 0.7))


def collide(place, rates, code, got, sums, low, high):
    return pl.pallas_call(
        collide_kernel,
        in_specs=[SMEM, SMEM, SMEM, ANY, ANY, ANY, ANY],
        out_specs=ANY,
        out_shape=made(16, 42, BS, LANES),
        scratch_shapes=[
            buffer(16, 3, BS, LANES),
            buffer(16, 3, LANES),
            buffer(16, 3, LANES),
            buffer(16, 8, SLOT_ROWS, LANES),
            buffer(42, BS, LANES),
            buffer(16, 42, BS, LANES),
            pltpu.SemaphoreType.DMA((3,)),
            pltpu.SemaphoreType.DMA((16,)),
            pltpu.SemaphoreType.DMA((16, 3)),
        ],
        compiler_params=room(60),
    )(place, rates, code, got, sums, low, high)


def finish_kernel(got, low_ref, high_ref, hydro, phase, n_ref, h_ref, p_ref, n_sem, h_sem, p_sem):
    row = lax.broadcasted_iota(jnp.int32, (BS, LANES), 0)

    def load(i):
        return pltpu.make_async_copy(got.at[i], n_ref.at[i], n_sem.at[i])

    def leave(i):
        for group in range(3):
            x = (i + group + 15) % 16
            comps = pl.ds(group * 9, 9)
            yield pltpu.make_async_copy(h_ref.at[i, comps], hydro.at[comps, x], h_sem.at[i, group])
            comps = pl.ds(group * 5, 5)
            yield pltpu.make_async_copy(p_ref.at[i, comps], phase.at[comps, x], p_sem.at[i, group])

    for i in range(16):
        load(i).start()

    @pl.loop(0, 16)
    def _(i):
        load(i).wait()
        for n, (kind, index, v) in enumerate(ORDER):
            value = n_ref[i, n]
            if v[1] == 1:
                face = low_ref[i, pl.ds(UP_FACE.index(n), 1), :]
                value = jnp.where(row == 0, face, pltpu.roll(value, 1, 0))
            elif v[1] == -1:
                face = high_ref[i, pl.ds(DOWN_FACE.index(n), 1), :]
                value = jnp.where(row == BS - 1, face, pltpu.roll(value, BS - 1, 0))
            (h_ref if kind == "h" else p_ref)[i, index] = value
        for copy in leave(i):
            copy.start()

    for i in range(16):
        for copy in leave(i):
            copy.wait()


def finish(got, low, high):
    return pl.pallas_call(
        finish_kernel,
        in_specs=[ANY, WHOLE, WHOLE],
        out_specs=[ANY, ANY],
        out_shape=[made(27, BS, BS, LANES), made(15, BS, BS, LANES)],
        scratch_shapes=[
            buffer(16, 42, BS, LANES),
            buffer(16, 27, BS, LANES),
            buffer(16, 15, BS, LANES),
            pltpu.SemaphoreType.DMA((16,)),
            pltpu.SemaphoreType.DMA((16, 3)),
            pltpu.SemaphoreType.DMA((16, 3)),
        ],
        compiler_params=room(24),
    )(got, low, high)


def swap_faces(upper, lower):
    size = lax.axis_size("gy")
    up = [(i, (i + 1) % size) for i in range(size)]
    down = [(j, i) for i, j in up]
    return lax.ppermute(upper, "gy", up), lax.ppermute(lower, "gy", down)


def on_device(hydro_old, phase_old, targets, flags, relax_rates):
    place = lax.axis_index("gx").astype(jnp.int32).reshape(1)
    slots = targets.shape[1]
    packed, place = pack(place, hydro_old[0], phase_old[0], targets, flags)
    got = lax.all_to_all(packed, "gx", split_axis=0, concat_axis=0, tiled=True)
    code, sums, up, down = survey(got, slots)
    low, high = swap_faces(up, down)
    send = collide(place, relax_rates, code, got, sums, low, high)
    final = lax.all_to_all(send, "gx", split_axis=0, concat_axis=0, tiled=True)
    upper = jnp.concatenate([final[:, a:b, BS - 1, :] for a, b in runs(UP_FACE)], axis=1)
    lower = jnp.concatenate([final[:, a:b, 0, :] for a, b in runs(DOWN_FACE)], axis=1)
    low, high = swap_faces(upper, lower)
    return tuple(finish(final, low, high))


def solution(mesh):
    in_specs = (
        P("gy", "gx", None, None),
        P("gy", "gx", None, None),
        P("gy", "gx"),
        P("gy", "gx"),
        P(),
    )
    out_specs = (P(None, "gx", "gy", None), P(None, "gx", "gy", None))
    return jax.shard_map(
        on_device, mesh=mesh, in_specs=in_specs, out_specs=out_specs, check_vma=False
    )
```

```python
import functools

import jax
import jax.numpy as jnp
import numpy as np
from jax import lax
from jax.experimental import pallas as pl
from jax.experimental.pallas import tpu as pltpu
from jax.sharding import PartitionSpec as P

BS = 16
BZ = 8
SLOT_ROWS = 88
AHEAD = 4
LANES = 128
MIB = 1024 * 1024
ANY = pl.BlockSpec(memory_space=pl.ANY)
SMEM = pl.BlockSpec(memory_space=pltpu.SMEM)
WHOLE = pl.BlockSpec(memory_space=pltpu.VMEM)


def room(mib):
    return pltpu.CompilerParams(vmem_limit_bytes=mib * MIB)


def buffer(*shape):
    return pltpu.VMEM(shape, jnp.float32)


def made(*shape):
    return jax.ShapeDtypeStruct(shape, jnp.float32)

FULL = [(a, b, c) for a in (-1, 0, 1) for b in (-1, 0, 1) for c in (-1, 0, 1)]
SMALL = [v for v in FULL if sum(map(abs, v)) != 2]
ORDER = sorted(
    [("h", q, v) for q, v in enumerate(FULL)] + [("p", k, v) for k, v in enumerate(SMALL)],
    key=lambda t: (t[2][0], t[0], t[2][1] if t[0] == "h" else -t[2][1], t[1]),
)
PLACE = {(kind, index): n for n, (kind, index, _) in enumerate(ORDER)}
UP_FACE = [n for n, t in enumerate(ORDER) if t[2][1] == 1]
DOWN_FACE = [n for n, t in enumerate(ORDER) if t[2][1] == -1]


def runs(places):
    out = []
    for n in places:
        if out and out[-1][1] == n:
            out[-1][1] = n + 1
        else:
            out.append([n, n + 1])
    return out


def pack_kernel(
    h_in, p_in, target_ref, flag_ref, out, h_ref, p_ref, o_ref, tag_ref, h_sem, p_sem, o_sem, tag_sem
):
    slots = target_ref.shape[1]

    def load(s):
        return (
            pltpu.make_async_copy(h_in.at[s], h_ref.at[s], h_sem.at[s]),
            pltpu.make_async_copy(p_in.at[s], p_ref.at[s], p_sem.at[s]),
        )

    def leave(s):
        rows = pl.ds(pl.multiple_of(s * SLOT_ROWS, 8), SLOT_ROWS)
        return pltpu.make_async_copy(o_ref.at[s], out.at[:, rows, :], o_sem.at[s])

    for s in range(slots):
        for copy in load(s):
            copy.start()
    tag_ref[:, 0:1, 0:slots] = jnp.broadcast_to(target_ref[...].astype(jnp.float32), (BS, 1, slots))
    tag_ref[:, 1:2, 0:slots] = jnp.broadcast_to(flag_ref[...].astype(jnp.float32), (BS, 1, slots))
    for i in range(BS):
        tag_ref[i, 2:3, :] = jnp.full((1, LANES), i, jnp.float32)
    tags = pltpu.make_async_copy(tag_ref, out.at[:, pl.ds(slots * SLOT_ROWS, 8), :], tag_sem)
    tags.start()

    @pl.loop(0, slots)
    def _(s):
        for copy in load(s):
            copy.wait()
        totals = [sum(p_ref[s, k, pl.ds(part * 8, 8), :] for k in range(15)) for part in range(4)]
        for part in range(4):
            rows = pl.ds(part * 8, 8)
            groups = [[h_ref[s, 4 * n + m, rows, :] for m in range(4)] for n in range(6)]
            groups += [[p_ref[s, 4 * n + m, rows, :] for m in range(4)] for n in range(3)]
            last_h = [h_ref[s, 24 + m, rows, :] for m in range(3)]
            last_p = [p_ref[s, 12 + m, rows, :] for m in range(3)]
            groups += [last_p + [beside(totals, part, -1)], last_h + [beside(totals, part, 1)]]
            for n, group in enumerate(groups):
                for m, value in enumerate(swap_bits(group, 0, 2)):
                    o_ref[s, part * 4 + m, pl.ds(n * 8, 8), :] = value
        leave(s).start()

    for s in range(slots):
        leave(s).wait()
    tags.wait()


def beside(totals, part, side):
    near, far = totals[part], totals[(part + side) % 4]
    row = lax.broadcasted_iota(jnp.int32, (8, LANES), 0)
    if side < 0:
        return jnp.where(row < 2, pltpu.roll(far, 2, 0), pltpu.roll(near, 2, 0))
    return jnp.where(row >= 6, pltpu.roll(far, 6, 0), pltpu.roll(near, 6, 0))


def pack(hydro, phase, targets, flags):
    slots = hydro.shape[0]
    return pl.pallas_call(
        pack_kernel,
        in_specs=[ANY, ANY, WHOLE, WHOLE],
        out_specs=ANY,
        out_shape=made(BS, slots * SLOT_ROWS + 8, LANES),
        scratch_shapes=[
            buffer(slots, 27, 32, LANES),
            buffer(slots, 15, 32, LANES),
            buffer(slots, BS, SLOT_ROWS, LANES),
            buffer(BS, 8, LANES),
            pltpu.SemaphoreType.DMA((slots,)),
            pltpu.SemaphoreType.DMA((slots,)),
            pltpu.SemaphoreType.DMA((slots,)),
            pltpu.SemaphoreType.DMA,
        ],
        compiler_params=room(60),
    )(hydro.reshape(slots, 27, 32, LANES), phase.reshape(slots, 15, 32, LANES), targets, flags)


def swap_bits(values, axis, unit):
    count = len(values)
    size = count * unit
    position = lax.broadcasted_iota(jnp.int32, (8, LANES), axis) // unit
    step = 1
    while step < count:
        high = (position & step) != 0
        fresh = list(values)
        for n in range(count):
            if n & step:
                continue
            a, b = values[n], values[n + step]
            fresh[n] = jnp.where(high, pltpu.roll(b, step * unit, axis), a)
            fresh[n + step] = jnp.where(high, b, pltpu.roll(a, size - step * unit, axis))
        values = fresh
        step *= 2
    return values


def swap_lanes(values):
    position = lax.broadcasted_iota(jnp.int32, (8, LANES), 1) // 16

    def skew(parts):
        for step in (1, 2, 4):
            high = (position & step) != 0
            parts = [jnp.where(high, parts[(n - step) % 8], parts[n]) for n in range(8)]
        return parts

    parts = skew([values[-n % 8] for n in range(8)])
    return skew([parts[0]] + [pltpu.roll(parts[n], LANES - 16 * n, 1) for n in range(1, 8)])


GROUPS = [[4 * n + m for m in range(4)] for n in range(6)]
GROUPS += [[27 + 4 * n + m for m in range(4)] for n in range(3)]
GROUPS += [[39, 40, 41, 42], [24, 25, 26, 43]]


def survey_kernel(
    got, code_ref, sum_ref, up_ref, down_ref, tag_ref, b_ref, code_s, tag_sem, b_sem, code_sem
):
    slots = b_ref.shape[0]
    tags = pltpu.make_async_copy(got.at[:, pl.ds(slots * SLOT_ROWS, 8), :], tag_ref, tag_sem)
    tags.start()
    loads = [
        pltpu.make_async_copy(got.at[:, pl.ds(t * SLOT_ROWS + 48, 40), :], b_ref.at[t], b_sem.at[t])
        for t in range(slots)
    ]
    for copy in loads:
        copy.start()
    tags.wait()

    row = lax.broadcasted_iota(jnp.int32, (8, LANES), 0)
    value = lax.broadcasted_iota(jnp.int32, (8, LANES), 1).astype(jnp.float32)
    code = jnp.zeros((8, LANES), jnp.float32)
    for half in range(2):
        label = tag_ref[pl.ds(half * 8, 8), 0, :]
        flag = tag_ref[pl.ds(half * 8, 8), 1, :]
        sender = ((row + half * 8) * 32).astype(jnp.float32)
        for t in range(slots):
            match = jnp.broadcast_to(label[:, t : t + 1], (8, LANES)) == value
            entry = sender + (2.0 * t + jnp.broadcast_to(flag[:, t : t + 1], (8, LANES)))
            code = code + jnp.where(match, entry, 0.0)
    code_ref[0:1, :] = jnp.sum(code, axis=0, keepdims=True).astype(jnp.int32)
    code_ref[1:2, :] = tag_ref[0, 2:3, :].astype(jnp.int32)
    table = pltpu.make_async_copy(code_ref, code_s, code_sem)
    table.start()
    table.wait()
    for copy in loads:
        copy.wait()

    @pl.loop(0, 16)
    def _(d):
        values = []
        for level in range(8):
            sender, slot, _ = decode(code_s[0, d * 8 + level])
            parts = [b_ref[slot, sender, pl.ds(n * 8, 8), :] for n in range(5)]
            own = parts[0] + parts[1] + parts[2] + jnp.where(row < 6, parts[3], 0.0)
            own = own + pltpu.roll(own, 2, 0)
            own = own + pltpu.roll(own, 4, 0)
            beyond = jnp.where(row < 4, pltpu.roll(parts[4], 4, 0), own)
            values.append(jnp.where(row < 2, pltpu.roll(parts[3], 2, 0), beyond))
        values = swap_bits(swap_lanes(values), 0, 1)
        for n in range(6):
            sum_ref[d, n // 2, pl.ds((n % 2) * 8, 8), :] = values[n]
        up_ref[d] = sum_ref[d, :, BS - 1, :]
        down_ref[d] = sum_ref[d, :, 0, :]


def decode(code):
    return lax.shift_right_logical(code, 5), lax.shift_right_logical(code, 1) & 15, code & 1


def survey(got, slots):
    return pl.pallas_call(
        survey_kernel,
        in_specs=[ANY],
        out_specs=[WHOLE, WHOLE, WHOLE, WHOLE],
        out_shape=[
            jax.ShapeDtypeStruct((2, LANES), jnp.int32),
            made(16, 3, BS, LANES),
            made(16, 3, LANES),
            made(16, 3, LANES),
        ],
        scratch_shapes=[
            buffer(16, 8, LANES),
            buffer(slots, 16, 40, LANES),
            pltpu.SMEM((2, LANES), jnp.int32),
            pltpu.SemaphoreType.DMA,
            pltpu.SemaphoreType.DMA((slots,)),
            pltpu.SemaphoreType.DMA,
        ],
        compiler_params=room(60),
    )(got)


def to_moments(f):
    f = list(f)
    for stride in (1, 3, 9):
        for n in range(27):
            if (n // stride) % 3 == 0:
                low, mid, high = f[n], f[n + stride], f[n + 2 * stride]
                both = low + high
                f[n], f[n + stride], f[n + 2 * stride] = both + mid, high - low, both
    return f


def from_moments(m):
    m = list(m)
    for stride in (1, 3, 9):
        for n in range(27):
            if (n // stride) % 3 == 0:
                zero, one, two = m[n], m[n + stride], m[n + 2 * stride]
                low, high = two - one, two + one
                m[n], m[n + stride], m[n + 2 * stride] = low, zero - (low + high), high
    return m


def equil_moments(pressure, velocity):
    x, y, z = velocity
    squares = (x * x, y * y, z * z)
    cross = {(1, 1, 0): x * y, (1, 0, 1): x * z, (0, 1, 1): y * z}
    third = pressure * (1.0 / 3.0)
    total = squares[0] + squares[1] + squares[2]
    out = [None] * 27
    for q in range(27):
        powers = (q // 9, q // 3 % 3, q % 3)
        ones = tuple(int(n == 1) for n in powers)
        scale = (1.0 / 3.0) ** sum(n == 2 for n in powers)
        if sum(ones) == 0:
            two = [squares[n] for n in range(3) if powers[n] == 2]
            value = pressure if not two else pressure + 3.0 * sum(two[1:], two[0])
            out[q] = value if scale == 1.0 else scale * value
        elif sum(ones) == 1:
            value = velocity[ones.index(1)]
            out[q] = value if scale == 1.0 else scale * value
        elif sum(ones) == 2:
            out[q] = cross[ones] if scale == 1.0 else scale * cross[ones]
        else:
            out[q] = 0.0
    return out


def weighted(v, table):
    return table[sum(map(abs, v))]


FULL_WEIGHT = [8.0 / 27.0, 2.0 / 27.0, 1.0 / 54.0, 1.0 / 216.0]
SMALL_WEIGHT = [2.0 / 9.0, 1.0 / 9.0, 0.0, 1.0 / 72.0]


def dot(v, parts):
    total = None
    for c, part in zip(v, parts):
        if c != 0:
            if total is None:
                total = part if c > 0 else -part
            else:
                total = total + part if c > 0 else total - part
    return total


def collide_kernel(
    rate_ref, code_ref, got, sums, low, high, out,
    sum_ref, low_ref, high_ref, b_ref, n_ref, o_ref, side_sem, b_sem, o_sem,
):
    place = code_ref[1, 0]
    sides = [
        pltpu.make_async_copy(a, b, side_sem.at[n])
        for n, (a, b) in enumerate(((sums, sum_ref), (low, low_ref), (high, high_ref)))
    ]

    def start(d):
        for level in range(8):
            sender, slot, _ = decode(code_ref[0, d * 8 + level])
            rows = pl.ds(pl.multiple_of(slot * SLOT_ROWS, 8), SLOT_ROWS)
            pltpu.make_async_copy(got.at[sender, rows, :], b_ref.at[d, level], b_sem.at[d]).start()

    def leave(d):
        left = jnp.where(place == 0, (d + 15) % 16, d)
        right = jnp.where(place == 15, (d + 1) % 16, d)
        for group, to in enumerate((left, d, right)):
            comps = pl.ds(group * 14, 14)
            yield pltpu.make_async_copy(o_ref.at[d, comps], out.at[to, comps], o_sem.at[d, group])

    for copy in sides:
        copy.start()
    for d in range(AHEAD):
        start(d)
    for copy in sides:
        copy.wait()

    @pl.loop(0, 16)
    def _(d):
        @pl.when(d + AHEAD < 16)
        def _():
            start(d + AHEAD)

        pltpu.make_async_copy(b_ref.at[d], b_ref.at[d], b_sem.at[d]).wait()
        for group, comps in enumerate(GROUPS):
            values = [b_ref[d, level, pl.ds(group * 8, 8), :] for level in range(8)]
            values = swap_bits(swap_lanes(values), 0, 1)
            for n in range(8):
                if comps[n // 2] < 42:
                    n_ref[comps[n // 2], pl.ds((n % 2) * 8, 8), :] = values[n]
        position = lax.broadcasted_iota(jnp.int32, (8, LANES), 1) // 16
        flag_line = jnp.zeros((8, LANES), jnp.float32)
        for level in range(8):
            flag = decode(code_ref[0, d * 8 + level])[2].astype(jnp.float32)
            flag_line = jnp.where(position == level, flag, flag_line)
        collide_plane(d, place, rate_ref, n_ref, sum_ref, low_ref, high_ref, flag_line, o_ref)
        for copy in leave(d):
            copy.start()

    for d in range(16):
        for copy in leave(d):
            copy.wait()


def collide_plane(d, place, rate_ref, n_ref, sum_ref, low_ref, high_ref, flag_line, out_ref):
    left = jnp.where(place == 0, (d + 15) % 16, d)
    right = jnp.where(place == 15, (d + 1) % 16, d)
    row = lax.broadcasted_iota(jnp.int32, (BS, LANES), 0)

    planes = []
    for index, which in ((left, 0), (d, 2), (right, 1)):
        centre = sum_ref[index, which]
        low = low_ref[index, pl.ds(which, 1), :]
        high = high_ref[index, pl.ds(which, 1), :]
        minus = jnp.where(row == 0, low, pltpu.roll(centre, 1, 0))
        plus = jnp.where(row == BS - 1, high, pltpu.roll(centre, BS - 1, 0))
        smooth_y = (2.0 / 3.0) * centre + (1.0 / 6.0) * (minus + plus)
        planes.append((smooth_y, plus - minus))

    def along_z(v):
        return pltpu.roll(v, LANES - 1, 1), pltpu.roll(v, 1, 1)

    def smooth_z(v):
        plus, minus = along_z(v)
        return (2.0 / 3.0) * v + (1.0 / 6.0) * (plus + minus)

    grad_x = 0.5 * smooth_z(planes[2][0] - planes[0][0])
    sides = planes[0][1] + planes[2][1]
    grad_y = 0.5 * smooth_z((2.0 / 3.0) * planes[1][1] + (1.0 / 6.0) * sides)
    sides = planes[0][0] + planes[2][0]
    plus, minus = along_z((2.0 / 3.0) * planes[1][0] + (1.0 / 6.0) * sides)
    grad_z = 0.5 * (plus - minus)

    for half in range(2):
        rows = slice(half * 8, half * 8 + 8)
        at = pl.ds(half * 8, 8)
        f = [n_ref[q, at, :] for q in range(27)]
        phase = sum_ref[d, 2, at, :]
        raw = to_moments(f)
        velocity = (raw[9], raw[3], raw[1])
        rest = equil_moments(raw[0], velocity)
        clipped = jnp.clip(phase, 0.0, 1.0)
        density = 0.001 + 0.999 * clipped
        dynamic = 1e-05 + 0.09999 * clipped
        shear = density / (0.5 * density + 3.0 * dynamic)
        scaled = [0.0] * 27
        for q in range(27):
            fold = 0.5 ** sum(n != 0 for n in (q // 9, q // 3 % 3, q % 3))
            rate = shear if q in (4, 10, 12) else rate_ref[q]
            scaled[q] = (rate * fold) * (raw[q] - rest[q])
        back = from_moments(scaled)

        def put(kind, index, v, value):
            out_ref[d, PLACE[kind, index], at, :] = value

        for q in range(27):
            put("h", q, FULL[q], f[q] - back[q])

        g = (grad_x[rows], grad_y[rows], grad_z[rows])
        scale = lax.rsqrt(g[0] * g[0] + g[1] * g[1] + g[2] * g[2] + 0.25)
        sharp = flag_line * (4.0 * phase * (1.0 - phase)) * scale
        drive = [3.0 * phase * velocity[n] + sharp * g[n] for n in range(3)]
        for k in range(15):
            w = weighted(SMALL[k], SMALL_WEIGHT)
            pop = n_ref[27 + k, at, :]
            push = dot(SMALL[k], drive)
            equil = w * (phase if push is None else phase + push)
            put("p", k, SMALL[k], pop - (pop - equil) * (1.0 / 0.7))


def collide(rates, code, got, sums, low, high):
    return pl.pallas_call(
        collide_kernel,
        in_specs=[SMEM, SMEM, ANY, ANY, ANY, ANY],
        out_specs=ANY,
        out_shape=made(16, 42, BS, LANES),
        scratch_shapes=[
            buffer(16, 3, BS, LANES),
            buffer(16, 3, LANES),
            buffer(16, 3, LANES),
            buffer(16, 8, SLOT_ROWS, LANES),
            buffer(42, BS, LANES),
            buffer(16, 42, BS, LANES),
            pltpu.SemaphoreType.DMA((3,)),
            pltpu.SemaphoreType.DMA((16,)),
            pltpu.SemaphoreType.DMA((16, 3)),
        ],
        compiler_params=room(60),
    )(rates, code, got, sums, low, high)


def finish_kernel(got, low, high, hydro, phase, low_ref, high_ref, n_ref, h_ref, p_ref, side_sem, n_sem, h_sem, p_sem):
    row = lax.broadcasted_iota(jnp.int32, (BS, LANES), 0)

    def load(i):
        return pltpu.make_async_copy(got.at[i], n_ref.at[i], n_sem.at[i])

    def leave(i):
        for group in range(3):
            x = (i + group + 15) % 16
            comps = pl.ds(group * 9, 9)
            yield pltpu.make_async_copy(h_ref.at[i, comps], hydro.at[comps, x], h_sem.at[i, group])
            comps = pl.ds(group * 5, 5)
            yield pltpu.make_async_copy(p_ref.at[i, comps], phase.at[comps, x], p_sem.at[i, group])

    sides = [
        pltpu.make_async_copy(a, b, side_sem.at[n])
        for n, (a, b) in enumerate(((low, low_ref), (high, high_ref)))
    ]
    for copy in sides:
        copy.start()
    for i in range(16):
        load(i).start()
    for copy in sides:
        copy.wait()

    @pl.loop(0, 16)
    def _(i):
        load(i).wait()
        for n, (kind, index, v) in enumerate(ORDER):
            value = n_ref[i, n]
            if v[1] == 1:
                face = low_ref[i, pl.ds(UP_FACE.index(n), 1), :]
                value = jnp.where(row == 0, face, pltpu.roll(value, 1, 0))
            elif v[1] == -1:
                face = high_ref[i, pl.ds(DOWN_FACE.index(n), 1), :]
                value = jnp.where(row == BS - 1, face, pltpu.roll(value, BS - 1, 0))
            if v[2] != 0:
                value = pltpu.roll(value, v[2] % LANES, 1)
            (h_ref if kind == "h" else p_ref)[i, index] = value
        for copy in leave(i):
            copy.start()

    for i in range(16):
        for copy in leave(i):
            copy.wait()


def finish(got, low, high):
    return pl.pallas_call(
        finish_kernel,
        in_specs=[ANY, ANY, ANY],
        out_specs=[ANY, ANY],
        out_shape=[made(27, BS, BS, LANES), made(15, BS, BS, LANES)],
        scratch_shapes=[
            buffer(16, 14, LANES),
            buffer(16, 14, LANES),
            buffer(16, 42, BS, LANES),
            buffer(16, 27, BS, LANES),
            buffer(16, 15, BS, LANES),
            pltpu.SemaphoreType.DMA((2,)),
            pltpu.SemaphoreType.DMA((16,)),
            pltpu.SemaphoreType.DMA((16, 3)),
            pltpu.SemaphoreType.DMA((16, 3)),
        ],
        compiler_params=room(24),
    )(got, low, high)


def swap_faces(upper, lower):
    size = lax.axis_size("gy")
    up = [(i, (i + 1) % size) for i in range(size)]
    down = [(j, i) for i, j in up]
    return lax.ppermute(upper, "gy", up), lax.ppermute(lower, "gy", down)


def on_device(hydro_old, phase_old, targets, flags, relax_rates):
    slots = targets.shape[1]
    packed = pack(hydro_old[0], phase_old[0], targets, flags)
    got = lax.all_to_all(packed, "gx", split_axis=0, concat_axis=0, tiled=True)
    code, sums, up, down = survey(got, slots)
    low, high = swap_faces(up, down)
    send = collide(relax_rates, code, got, sums, low, high)
    final = lax.all_to_all(send, "gx", split_axis=0, concat_axis=0, tiled=True)
    upper = jnp.concatenate([final[:, a:b, BS - 1, :] for a, b in runs(UP_FACE)], axis=1)
    lower = jnp.concatenate([final[:, a:b, 0, :] for a, b in runs(DOWN_FACE)], axis=1)
    low, high = swap_faces(upper, lower)
    return tuple(finish(final, low, high))


def solution(mesh):
    in_specs = (
        P("gy", "gx", None, None),
        P("gy", "gx", None, None),
        P("gy", "gx"),
        P("gy", "gx"),
        P(),
    )
    out_specs = (P(None, "gx", "gy", None), P(None, "gx", "gy", None))
    return jax.shard_map(
        on_device, mesh=mesh, in_specs=in_specs, out_specs=out_specs, check_vma=False
    )
```

```python
import functools

import jax
import jax.numpy as jnp
import numpy as np
from jax import lax
from jax.experimental import pallas as pl
from jax.experimental.pallas import tpu as pltpu
from jax.sharding import PartitionSpec as P

BS = 16
BZ = 8
SLOT_ROWS = 88
AHEAD = 4
LANES = 128
MIB = 1024 * 1024
ANY = pl.BlockSpec(memory_space=pl.ANY)
SMEM = pl.BlockSpec(memory_space=pltpu.SMEM)
WHOLE = pl.BlockSpec(memory_space=pltpu.VMEM)


def room(mib):
    return pltpu.CompilerParams(vmem_limit_bytes=mib * MIB)


def buffer(*shape):
    return pltpu.VMEM(shape, jnp.float32)


def made(*shape):
    return jax.ShapeDtypeStruct(shape, jnp.float32)

FULL = [(a, b, c) for a in (-1, 0, 1) for b in (-1, 0, 1) for c in (-1, 0, 1)]
SMALL = [v for v in FULL if sum(map(abs, v)) != 2]
ORDER = sorted(
    [("h", q, v) for q, v in enumerate(FULL)] + [("p", k, v) for k, v in enumerate(SMALL)],
    key=lambda t: (t[2][0], t[0], t[2][1] if t[0] == "h" else -t[2][1], t[1]),
)
PLACE = {(kind, index): n for n, (kind, index, _) in enumerate(ORDER)}
UP_FACE = [n for n, t in enumerate(ORDER) if t[2][1] == 1]
DOWN_FACE = [n for n, t in enumerate(ORDER) if t[2][1] == -1]


def runs(places):
    out = []
    for n in places:
        if out and out[-1][1] == n:
            out[-1][1] = n + 1
        else:
            out.append([n, n + 1])
    return out


def pack_kernel(
    h_in, p_in, target_ref, flag_ref, out, h_ref, p_ref, o_ref, tag_ref, h_sem, p_sem, o_sem, tag_sem
):
    slots = target_ref.shape[1]

    def load(s):
        return (
            pltpu.make_async_copy(h_in.at[s], h_ref.at[s], h_sem.at[s]),
            pltpu.make_async_copy(p_in.at[s], p_ref.at[s], p_sem.at[s]),
        )

    def leave(s):
        rows = pl.ds(pl.multiple_of(s * SLOT_ROWS, 8), SLOT_ROWS)
        return pltpu.make_async_copy(o_ref.at[s], out.at[:, rows, :], o_sem.at[s])

    for s in range(slots):
        for copy in load(s):
            copy.start()
    tag_ref[:, 0:1, 0:slots] = jnp.broadcast_to(target_ref[...].astype(jnp.float32), (BS, 1, slots))
    tag_ref[:, 1:2, 0:slots] = jnp.broadcast_to(flag_ref[...].astype(jnp.float32), (BS, 1, slots))
    for i in range(BS):
        tag_ref[i, 2:3, :] = jnp.full((1, LANES), i, jnp.float32)
    tags = pltpu.make_async_copy(tag_ref, out.at[:, pl.ds(slots * SLOT_ROWS, 8), :], tag_sem)
    tags.start()

    @pl.loop(0, slots)
    def _(s):
        for copy in load(s):
            copy.wait()
        totals = [sum(p_ref[s, k, pl.ds(part * 8, 8), :] for k in range(15)) for part in range(4)]
        for part in range(4):
            rows = pl.ds(part * 8, 8)
            groups = [[h_ref[s, 4 * n + m, rows, :] for m in range(4)] for n in range(6)]
            groups += [[p_ref[s, 4 * n + m, rows, :] for m in range(4)] for n in range(3)]
            last_h = [h_ref[s, 24 + m, rows, :] for m in range(3)]
            last_p = [p_ref[s, 12 + m, rows, :] for m in range(3)]
            groups += [last_p + [beside(totals, part, -1)], last_h + [beside(totals, part, 1)]]
            for n, group in enumerate(groups):
                for m, value in enumerate(swap_bits(group, 0, 2)):
                    o_ref[s, part * 4 + m, pl.ds(n * 8, 8), :] = value
        leave(s).start()

    for s in range(slots):
        leave(s).wait()
    tags.wait()


def beside(totals, part, side):
    near, far = totals[part], totals[(part + side) % 4]
    row = lax.broadcasted_iota(jnp.int32, (8, LANES), 0)
    if side < 0:
        return jnp.where(row < 2, pltpu.roll(far, 2, 0), pltpu.roll(near, 2, 0))
    return jnp.where(row >= 6, pltpu.roll(far, 6, 0), pltpu.roll(near, 6, 0))


def pack(hydro, phase, targets, flags):
    slots = hydro.shape[0]
    return pl.pallas_call(
        pack_kernel,
        in_specs=[ANY, ANY, WHOLE, WHOLE],
        out_specs=ANY,
        out_shape=made(BS, slots * SLOT_ROWS + 8, LANES),
        scratch_shapes=[
            buffer(slots, 27, 32, LANES),
            buffer(slots, 15, 32, LANES),
            buffer(slots, BS, SLOT_ROWS, LANES),
            buffer(BS, 8, LANES),
            pltpu.SemaphoreType.DMA((slots,)),
            pltpu.SemaphoreType.DMA((slots,)),
            pltpu.SemaphoreType.DMA((slots,)),
            pltpu.SemaphoreType.DMA,
        ],
        compiler_params=room(60),
    )(hydro.reshape(slots, 27, 32, LANES), phase.reshape(slots, 15, 32, LANES), targets, flags)


def swap_bits(values, axis, unit):
    count = len(values)
    size = count * unit
    position = lax.broadcasted_iota(jnp.int32, (8, LANES), axis) // unit
    step = 1
    while step < count:
        high = (position & step) != 0
        fresh = list(values)
        for n in range(count):
            if n & step:
                continue
            a, b = values[n], values[n + step]
            fresh[n] = jnp.where(high, pltpu.roll(b, step * unit, axis), a)
            fresh[n + step] = jnp.where(high, b, pltpu.roll(a, size - step * unit, axis))
        values = fresh
        step *= 2
    return values


def swap_lanes(values):
    position = lax.broadcasted_iota(jnp.int32, (8, LANES), 1) // 16

    def skew(parts):
        for step in (1, 2, 4):
            high = (position & step) != 0
            parts = [jnp.where(high, parts[(n - step) % 8], parts[n]) for n in range(8)]
        return parts

    parts = skew([values[-n % 8] for n in range(8)])
    return skew([parts[0]] + [pltpu.roll(parts[n], LANES - 16 * n, 1) for n in range(1, 8)])


GROUPS = [[4 * n + m for m in range(4)] for n in range(6)]
GROUPS += [[27 + 4 * n + m for m in range(4)] for n in range(3)]
GROUPS += [[39, 40, 41, 42], [24, 25, 26, 43]]


def survey_kernel(
    got, code_ref, sum_ref, up_ref, down_ref, tag_ref, b_ref, code_s, tag_sem, b_sem, code_sem
):
    slots = b_ref.shape[0]
    tags = pltpu.make_async_copy(got.at[:, pl.ds(slots * SLOT_ROWS, 8), :], tag_ref, tag_sem)
    tags.start()
    loads = [
        pltpu.make_async_copy(got.at[:, pl.ds(t * SLOT_ROWS + 48, 40), :], b_ref.at[t], b_sem.at[t])
        for t in range(slots)
    ]
    for copy in loads:
        copy.start()
    tags.wait()

    row = lax.broadcasted_iota(jnp.int32, (8, LANES), 0)
    value = lax.broadcasted_iota(jnp.int32, (8, LANES), 1).astype(jnp.float32)
    code = jnp.zeros((8, LANES), jnp.float32)
    for half in range(2):
        label = tag_ref[pl.ds(half * 8, 8), 0, :]
        flag = tag_ref[pl.ds(half * 8, 8), 1, :]
        sender = ((row + half * 8) * 32).astype(jnp.float32)
        for t in range(slots):
            match = jnp.broadcast_to(label[:, t : t + 1], (8, LANES)) == value
            entry = sender + (2.0 * t + jnp.broadcast_to(flag[:, t : t + 1], (8, LANES)))
            code = code + jnp.where(match, entry, 0.0)
    code_ref[0:1, :] = jnp.sum(code, axis=0, keepdims=True).astype(jnp.int32)
    code_ref[1:2, :] = tag_ref[0, 2:3, :].astype(jnp.int32)
    table = pltpu.make_async_copy(code_ref, code_s, code_sem)
    table.start()
    table.wait()
    for copy in loads:
        copy.wait()

    @pl.loop(0, 16, unroll=4)
    def _(d):
        values = []
        for level in range(8):
            sender, slot, _ = decode(code_s[0, d * 8 + level])
            parts = [b_ref[slot, sender, pl.ds(n * 8, 8), :] for n in range(5)]
            own = parts[0] + parts[1] + parts[2] + jnp.where(row < 6, parts[3], 0.0)
            own = own + pltpu.roll(own, 2, 0)
            own = own + pltpu.roll(own, 4, 0)
            beyond = jnp.where(row < 4, pltpu.roll(parts[4], 4, 0), own)
            values.append(jnp.where(row < 2, pltpu.roll(parts[3], 2, 0), beyond))
        values = swap_bits(swap_lanes(values), 0, 1)
        for n in range(6):
            sum_ref[d, n // 2, pl.ds((n % 2) * 8, 8), :] = values[n]
        up_ref[d] = sum_ref[d, :, BS - 1, :]
        down_ref[d] = sum_ref[d, :, 0, :]


def decode(code):
    return lax.shift_right_logical(code, 5), lax.shift_right_logical(code, 1) & 15, code & 1


def survey(got, slots):
    return pl.pallas_call(
        survey_kernel,
        in_specs=[ANY],
        out_specs=[WHOLE, WHOLE, WHOLE, WHOLE],
        out_shape=[
            jax.ShapeDtypeStruct((2, LANES), jnp.int32),
            made(16, 3, BS, LANES),
            made(16, 3, LANES),
            made(16, 3, LANES),
        ],
        scratch_shapes=[
            buffer(16, 8, LANES),
            buffer(slots, 16, 40, LANES),
            pltpu.SMEM((2, LANES), jnp.int32),
            pltpu.SemaphoreType.DMA,
            pltpu.SemaphoreType.DMA((slots,)),
            pltpu.SemaphoreType.DMA,
        ],
        compiler_params=room(60),
    )(got)


def to_moments(f):
    f = list(f)
    for stride in (1, 3, 9):
        for n in range(27):
            if (n // stride) % 3 == 0:
                low, mid, high = f[n], f[n + stride], f[n + 2 * stride]
                both = low + high
                f[n], f[n + stride], f[n + 2 * stride] = both + mid, high - low, both
    return f


def from_moments(m):
    m = list(m)
    for stride in (1, 3, 9):
        for n in range(27):
            if (n // stride) % 3 == 0:
                zero, one, two = m[n], m[n + stride], m[n + 2 * stride]
                low, high = two - one, two + one
                m[n], m[n + stride], m[n + 2 * stride] = low, zero - (low + high), high
    return m


def equil_moments(pressure, velocity):
    x, y, z = velocity
    squares = (x * x, y * y, z * z)
    cross = {(1, 1, 0): x * y, (1, 0, 1): x * z, (0, 1, 1): y * z}
    third = pressure * (1.0 / 3.0)
    total = squares[0] + squares[1] + squares[2]
    out = [None] * 27
    for q in range(27):
        powers = (q // 9, q // 3 % 3, q % 3)
        ones = tuple(int(n == 1) for n in powers)
        scale = (1.0 / 3.0) ** sum(n == 2 for n in powers)
        if sum(ones) == 0:
            two = [squares[n] for n in range(3) if powers[n] == 2]
            value = pressure if not two else pressure + 3.0 * sum(two[1:], two[0])
            out[q] = value if scale == 1.0 else scale * value
        elif sum(ones) == 1:
            value = velocity[ones.index(1)]
            out[q] = value if scale == 1.0 else scale * value
        elif sum(ones) == 2:
            out[q] = cross[ones] if scale == 1.0 else scale * cross[ones]
        else:
            out[q] = 0.0
    return out


def weighted(v, table):
    return table[sum(map(abs, v))]


FULL_WEIGHT = [8.0 / 27.0, 2.0 / 27.0, 1.0 / 54.0, 1.0 / 216.0]
SMALL_WEIGHT = [2.0 / 9.0, 1.0 / 9.0, 0.0, 1.0 / 72.0]


def dot(v, parts):
    total = None
    for c, part in zip(v, parts):
        if c != 0:
            if total is None:
                total = part if c > 0 else -part
            else:
                total = total + part if c > 0 else total - part
    return total


def collide_kernel(
    rate_ref, code_ref, got, sums, low, high, out,
    sum_ref, low_ref, high_ref, b_ref, n_ref, o_ref, side_sem, b_sem, o_sem,
):
    place = code_ref[1, 0]
    sides = [
        pltpu.make_async_copy(a, b, side_sem.at[n])
        for n, (a, b) in enumerate(((sums, sum_ref), (low, low_ref), (high, high_ref)))
    ]

    def start(d):
        for level in range(8):
            sender, slot, _ = decode(code_ref[0, d * 8 + level])
            rows = pl.ds(pl.multiple_of(slot * SLOT_ROWS, 8), SLOT_ROWS)
            pltpu.make_async_copy(got.at[sender, rows, :], b_ref.at[d, level], b_sem.at[d]).start()

    def leave(d):
        left = jnp.where(place == 0, (d + 15) % 16, d)
        right = jnp.where(place == 15, (d + 1) % 16, d)
        for group, to in enumerate((left, d, right)):
            comps = pl.ds(group * 14, 14)
            yield pltpu.make_async_copy(o_ref.at[d, comps], out.at[to, comps], o_sem.at[d, group])

    for copy in sides:
        copy.start()
    for d in range(AHEAD):
        start(d)
    for copy in sides:
        copy.wait()

    @pl.loop(0, 16)
    def _(d):
        @pl.when(d + AHEAD < 16)
        def _():
            start(d + AHEAD)

        pltpu.make_async_copy(b_ref.at[d], b_ref.at[d], b_sem.at[d]).wait()
        for group, comps in enumerate(GROUPS):
            values = [b_ref[d, level, pl.ds(group * 8, 8), :] for level in range(8)]
            values = swap_bits(swap_lanes(values), 0, 1)
            for n in range(8):
                if comps[n // 2] < 42:
                    n_ref[comps[n // 2], pl.ds((n % 2) * 8, 8), :] = values[n]
        position = lax.broadcasted_iota(jnp.int32, (8, LANES), 1) // 16
        flag_line = jnp.zeros((8, LANES), jnp.float32)
        for level in range(8):
            flag = decode(code_ref[0, d * 8 + level])[2].astype(jnp.float32)
            flag_line = jnp.where(position == level, flag, flag_line)
        collide_plane(d, place, rate_ref, n_ref, sum_ref, low_ref, high_ref, flag_line, o_ref)
        for copy in leave(d):
            copy.start()

    for d in range(16):
        for copy in leave(d):
            copy.wait()


def collide_plane(d, place, rate_ref, n_ref, sum_ref, low_ref, high_ref, flag_line, out_ref):
    left = jnp.where(place == 0, (d + 15) % 16, d)
    right = jnp.where(place == 15, (d + 1) % 16, d)
    row = lax.broadcasted_iota(jnp.int32, (BS, LANES), 0)

    planes = []
    for index, which in ((left, 0), (d, 2), (right, 1)):
        centre = sum_ref[index, which]
        low = low_ref[index, pl.ds(which, 1), :]
        high = high_ref[index, pl.ds(which, 1), :]
        minus = jnp.where(row == 0, low, pltpu.roll(centre, 1, 0))
        plus = jnp.where(row == BS - 1, high, pltpu.roll(centre, BS - 1, 0))
        smooth_y = (2.0 / 3.0) * centre + (1.0 / 6.0) * (minus + plus)
        planes.append((smooth_y, plus - minus))

    def along_z(v):
        return pltpu.roll(v, LANES - 1, 1), pltpu.roll(v, 1, 1)

    def smooth_z(v):
        plus, minus = along_z(v)
        return (2.0 / 3.0) * v + (1.0 / 6.0) * (plus + minus)

    grad_x = 0.5 * smooth_z(planes[2][0] - planes[0][0])
    sides = planes[0][1] + planes[2][1]
    grad_y = 0.5 * smooth_z((2.0 / 3.0) * planes[1][1] + (1.0 / 6.0) * sides)
    sides = planes[0][0] + planes[2][0]
    plus, minus = along_z((2.0 / 3.0) * planes[1][0] + (1.0 / 6.0) * sides)
    grad_z = 0.5 * (plus - minus)

    for half in range(2):
        rows = slice(half * 8, half * 8 + 8)
        at = pl.ds(half * 8, 8)
        f = [n_ref[q, at, :] for q in range(27)]
        phase = sum_ref[d, 2, at, :]
        raw = to_moments(f)
        velocity = (raw[9], raw[3], raw[1])
        rest = equil_moments(raw[0], velocity)
        clipped = jnp.clip(phase, 0.0, 1.0)
        density = 0.001 + 0.999 * clipped
        dynamic = 1e-05 + 0.09999 * clipped
        shear = density / (0.5 * density + 3.0 * dynamic)
        scaled = [0.0] * 27
        for q in range(27):
            fold = 0.5 ** sum(n != 0 for n in (q // 9, q // 3 % 3, q % 3))
            rate = shear if q in (4, 10, 12) else rate_ref[q]
            scaled[q] = (rate * fold) * (raw[q] - rest[q])
        back = from_moments(scaled)

        def put(kind, index, v, value):
            out_ref[d, PLACE[kind, index], at, :] = value

        for q in range(27):
            put("h", q, FULL[q], f[q] - back[q])

        g = (grad_x[rows], grad_y[rows], grad_z[rows])
        scale = lax.rsqrt(g[0] * g[0] + g[1] * g[1] + g[2] * g[2] + 0.25)
        sharp = flag_line * (4.0 * phase * (1.0 - phase)) * scale
        drive = [3.0 * phase * velocity[n] + sharp * g[n] for n in range(3)]
        for k in range(15):
            w = weighted(SMALL[k], SMALL_WEIGHT)
            pop = n_ref[27 + k, at, :]
            push = dot(SMALL[k], drive)
            equil = w * (phase if push is None else phase + push)
            put("p", k, SMALL[k], pop - (pop - equil) * (1.0 / 0.7))


def collide(rates, code, got, sums, low, high):
    return pl.pallas_call(
        collide_kernel,
        in_specs=[SMEM, SMEM, ANY, ANY, ANY, ANY],
        out_specs=ANY,
        out_shape=made(16, 42, BS, LANES),
        scratch_shapes=[
            buffer(16, 3, BS, LANES),
            buffer(16, 3, LANES),
            buffer(16, 3, LANES),
            buffer(16, 8, SLOT_ROWS, LANES),
            buffer(42, BS, LANES),
            buffer(16, 42, BS, LANES),
            pltpu.SemaphoreType.DMA((3,)),
            pltpu.SemaphoreType.DMA((16,)),
            pltpu.SemaphoreType.DMA((16, 3)),
        ],
        compiler_params=room(60),
    )(rates, code, got, sums, low, high)


def finish_kernel(got, low, high, hydro, phase, low_ref, high_ref, n_ref, h_ref, p_ref, side_sem, n_sem, h_sem, p_sem):
    row = lax.broadcasted_iota(jnp.int32, (BS, LANES), 0)

    def load(i):
        return pltpu.make_async_copy(got.at[i], n_ref.at[i], n_sem.at[i])

    def leave(i):
        for group in range(3):
            x = (i + group + 15) % 16
            comps = pl.ds(group * 9, 9)
            yield pltpu.make_async_copy(h_ref.at[i, comps], hydro.at[comps, x], h_sem.at[i, group])
            comps = pl.ds(group * 5, 5)
            yield pltpu.make_async_copy(p_ref.at[i, comps], phase.at[comps, x], p_sem.at[i, group])

    sides = [
        pltpu.make_async_copy(a, b, side_sem.at[n])
        for n, (a, b) in enumerate(((low, low_ref), (high, high_ref)))
    ]
    for copy in sides:
        copy.start()
    for i in range(16):
        load(i).start()
    for copy in sides:
        copy.wait()

    @pl.loop(0, 16)
    def _(i):
        load(i).wait()
        for n, (kind, index, v) in enumerate(ORDER):
            value = n_ref[i, n]
            if v[1] == 1:
                face = low_ref[i, pl.ds(UP_FACE.index(n), 1), :]
                value = jnp.where(row == 0, face, pltpu.roll(value, 1, 0))
            elif v[1] == -1:
                face = high_ref[i, pl.ds(DOWN_FACE.index(n), 1), :]
                value = jnp.where(row == BS - 1, face, pltpu.roll(value, BS - 1, 0))
            if v[2] != 0:
                value = pltpu.roll(value, v[2] % LANES, 1)
            (h_ref if kind == "h" else p_ref)[i, index] = value
        for copy in leave(i):
            copy.start()

    for i in range(16):
        for copy in leave(i):
            copy.wait()


def finish(got, low, high):
    return pl.pallas_call(
        finish_kernel,
        in_specs=[ANY, ANY, ANY],
        out_specs=[ANY, ANY],
        out_shape=[made(27, BS, BS, LANES), made(15, BS, BS, LANES)],
        scratch_shapes=[
            buffer(16, 14, LANES),
            buffer(16, 14, LANES),
            buffer(16, 42, BS, LANES),
            buffer(16, 27, BS, LANES),
            buffer(16, 15, BS, LANES),
            pltpu.SemaphoreType.DMA((2,)),
            pltpu.SemaphoreType.DMA((16,)),
            pltpu.SemaphoreType.DMA((16, 3)),
            pltpu.SemaphoreType.DMA((16, 3)),
        ],
        compiler_params=room(24),
    )(got, low, high)


def swap_faces(upper, lower):
    size = lax.axis_size("gy")
    up = [(i, (i + 1) % size) for i in range(size)]
    down = [(j, i) for i, j in up]
    return lax.ppermute(upper, "gy", up), lax.ppermute(lower, "gy", down)


def on_device(hydro_old, phase_old, targets, flags, relax_rates):
    slots = targets.shape[1]
    packed = pack(hydro_old[0], phase_old[0], targets, flags)
    got = lax.all_to_all(packed, "gx", split_axis=0, concat_axis=0, tiled=True)
    code, sums, up, down = survey(got, slots)
    low, high = swap_faces(up, down)
    send = collide(relax_rates, code, got, sums, low, high)
    final = lax.all_to_all(send, "gx", split_axis=0, concat_axis=0, tiled=True)
    upper = jnp.concatenate([final[:, a:b, BS - 1, :] for a, b in runs(UP_FACE)], axis=1)
    lower = jnp.concatenate([final[:, a:b, 0, :] for a, b in runs(DOWN_FACE)], axis=1)
    low, high = swap_faces(upper, lower)
    return tuple(finish(final, low, high))


def solution(mesh):
    in_specs = (
        P("gy", "gx", None, None),
        P("gy", "gx", None, None),
        P("gy", "gx"),
        P("gy", "gx"),
        P(),
    )
    out_specs = (P(None, "gx", "gy", None), P(None, "gx", "gy", None))
    return jax.shard_map(
        on_device, mesh=mesh, in_specs=in_specs, out_specs=out_specs, check_vma=False
    )
```

```python
import functools

import jax
import jax.numpy as jnp
import numpy as np
from jax import lax
from jax.experimental import pallas as pl
from jax.experimental.pallas import tpu as pltpu
from jax.sharding import PartitionSpec as P

BS = 16
BZ = 8
SLOT_ROWS = 88
AHEAD = 4
LANES = 128
MIB = 1024 * 1024
ANY = pl.BlockSpec(memory_space=pl.ANY)
SMEM = pl.BlockSpec(memory_space=pltpu.SMEM)
WHOLE = pl.BlockSpec(memory_space=pltpu.VMEM)


def room(mib):
    return pltpu.CompilerParams(vmem_limit_bytes=mib * MIB)


def buffer(*shape):
    return pltpu.VMEM(shape, jnp.float32)


def made(*shape):
    return jax.ShapeDtypeStruct(shape, jnp.float32)

FULL = [(a, b, c) for a in (-1, 0, 1) for b in (-1, 0, 1) for c in (-1, 0, 1)]
SMALL = [v for v in FULL if sum(map(abs, v)) != 2]
ORDER = sorted(
    [("h", q, v) for q, v in enumerate(FULL)] + [("p", k, v) for k, v in enumerate(SMALL)],
    key=lambda t: (t[2][0], t[0], t[2][1] if t[0] == "h" else -t[2][1], t[1]),
)
PLACE = {(kind, index): n for n, (kind, index, _) in enumerate(ORDER)}
UP_FACE = [n for n, t in enumerate(ORDER) if t[2][1] == 1]
DOWN_FACE = [n for n, t in enumerate(ORDER) if t[2][1] == -1]


def runs(places):
    out = []
    for n in places:
        if out and out[-1][1] == n:
            out[-1][1] = n + 1
        else:
            out.append([n, n + 1])
    return out


def pack_kernel(
    h_in, p_in, target_ref, flag_ref, out, h_ref, p_ref, o_ref, tag_ref, h_sem, p_sem, o_sem, tag_sem
):
    slots = target_ref.shape[1]

    def load(s):
        return (
            pltpu.make_async_copy(h_in.at[s], h_ref.at[s], h_sem.at[s]),
            pltpu.make_async_copy(p_in.at[s], p_ref.at[s], p_sem.at[s]),
        )

    def leave(s):
        rows = pl.ds(pl.multiple_of(s * SLOT_ROWS, 8), SLOT_ROWS)
        return pltpu.make_async_copy(o_ref.at[s], out.at[:, rows, :], o_sem.at[s])

    for s in range(slots):
        for copy in load(s):
            copy.start()
    tag_ref[:, 0:1, 0:slots] = jnp.broadcast_to(target_ref[...].astype(jnp.float32), (BS, 1, slots))
    tag_ref[:, 1:2, 0:slots] = jnp.broadcast_to(flag_ref[...].astype(jnp.float32), (BS, 1, slots))
    for i in range(BS):
        tag_ref[i, 2:3, :] = jnp.full((1, LANES), i, jnp.float32)
    tags = pltpu.make_async_copy(tag_ref, out.at[:, pl.ds(slots * SLOT_ROWS, 8), :], tag_sem)
    tags.start()

    @pl.loop(0, slots)
    def _(s):
        for copy in load(s):
            copy.wait()
        totals = [sum(p_ref[s, k, pl.ds(part * 8, 8), :] for k in range(15)) for part in range(4)]
        for part in range(4):
            rows = pl.ds(part * 8, 8)
            groups = [[h_ref[s, 4 * n + m, rows, :] for m in range(4)] for n in range(6)]
            groups += [[p_ref[s, 4 * n + m, rows, :] for m in range(4)] for n in range(3)]
            last_h = [h_ref[s, 24 + m, rows, :] for m in range(3)]
            last_p = [p_ref[s, 12 + m, rows, :] for m in range(3)]
            groups += [last_p + [beside(totals, part, -1)], last_h + [beside(totals, part, 1)]]
            for n, group in enumerate(groups):
                for m, value in enumerate(swap_bits(group, 0, 2)):
                    o_ref[s, part * 4 + m, pl.ds(n * 8, 8), :] = value
        leave(s).start()

    for s in range(slots):
        leave(s).wait()
    tags.wait()


def beside(totals, part, side):
    near, far = totals[part], totals[(part + side) % 4]
    row = lax.broadcasted_iota(jnp.int32, (8, LANES), 0)
    if side < 0:
        return jnp.where(row < 2, pltpu.roll(far, 2, 0), pltpu.roll(near, 2, 0))
    return jnp.where(row >= 6, pltpu.roll(far, 6, 0), pltpu.roll(near, 6, 0))


def pack(hydro, phase, targets, flags):
    slots = hydro.shape[0]
    return pl.pallas_call(
        pack_kernel,
        in_specs=[ANY, ANY, WHOLE, WHOLE],
        out_specs=ANY,
        out_shape=made(BS, slots * SLOT_ROWS + 8, LANES),
        scratch_shapes=[
            buffer(slots, 27, 32, LANES),
            buffer(slots, 15, 32, LANES),
            buffer(slots, BS, SLOT_ROWS, LANES),
            buffer(BS, 8, LANES),
            pltpu.SemaphoreType.DMA((slots,)),
            pltpu.SemaphoreType.DMA((slots,)),
            pltpu.SemaphoreType.DMA((slots,)),
            pltpu.SemaphoreType.DMA,
        ],
        compiler_params=room(60),
    )(hydro.reshape(slots, 27, 32, LANES), phase.reshape(slots, 15, 32, LANES), targets, flags)


def swap_bits(values, axis, unit):
    count = len(values)
    size = count * unit
    position = lax.broadcasted_iota(jnp.int32, (8, LANES), axis) // unit
    step = 1
    while step < count:
        high = (position & step) != 0
        fresh = list(values)
        for n in range(count):
            if n & step:
                continue
            a, b = values[n], values[n + step]
            fresh[n] = jnp.where(high, pltpu.roll(b, step * unit, axis), a)
            fresh[n + step] = jnp.where(high, b, pltpu.roll(a, size - step * unit, axis))
        values = fresh
        step *= 2
    return values


def swap_lanes(values):
    position = lax.broadcasted_iota(jnp.int32, (8, LANES), 1) // 16

    def skew(parts):
        for step in (1, 2, 4):
            high = (position & step) != 0
            parts = [jnp.where(high, parts[(n - step) % 8], parts[n]) for n in range(8)]
        return parts

    parts = skew([values[-n % 8] for n in range(8)])
    return skew([parts[0]] + [pltpu.roll(parts[n], LANES - 16 * n, 1) for n in range(1, 8)])


GROUPS = [[4 * n + m for m in range(4)] for n in range(6)]
GROUPS += [[27 + 4 * n + m for m in range(4)] for n in range(3)]
GROUPS += [[39, 40, 41, 42], [24, 25, 26, 43]]


def survey_kernel(
    got, code_ref, sum_ref, up_ref, down_ref, tag_ref, b_ref, code_s, tag_sem, b_sem, code_sem
):
    slots = b_ref.shape[0]
    tags = pltpu.make_async_copy(got.at[:, pl.ds(slots * SLOT_ROWS, 8), :], tag_ref, tag_sem)
    tags.start()
    loads = [
        pltpu.make_async_copy(got.at[:, pl.ds(t * SLOT_ROWS + 48, 40), :], b_ref.at[t], b_sem.at[t])
        for t in range(slots)
    ]
    for copy in loads:
        copy.start()
    tags.wait()

    row = lax.broadcasted_iota(jnp.int32, (8, LANES), 0)
    value = lax.broadcasted_iota(jnp.int32, (8, LANES), 1).astype(jnp.float32)
    code = jnp.zeros((8, LANES), jnp.float32)
    for half in range(2):
        label = tag_ref[pl.ds(half * 8, 8), 0, :]
        flag = tag_ref[pl.ds(half * 8, 8), 1, :]
        sender = ((row + half * 8) * 32).astype(jnp.float32)
        for t in range(slots):
            match = jnp.broadcast_to(label[:, t : t + 1], (8, LANES)) == value
            entry = sender + (2.0 * t + jnp.broadcast_to(flag[:, t : t + 1], (8, LANES)))
            code = code + jnp.where(match, entry, 0.0)
    code_ref[0:1, :] = jnp.sum(code, axis=0, keepdims=True).astype(jnp.int32)
    code_ref[1:2, :] = tag_ref[0, 2:3, :].astype(jnp.int32)
    table = pltpu.make_async_copy(code_ref, code_s, code_sem)
    table.start()
    table.wait()
    for copy in loads:
        copy.wait()

    @pl.loop(0, 16, unroll=4)
    def _(d):
        values = []
        for level in range(8):
            sender, slot, _ = decode(code_s[0, d * 8 + level])
            parts = [b_ref[slot, sender, pl.ds(n * 8, 8), :] for n in range(5)]
            own = parts[0] + parts[1] + parts[2] + jnp.where(row < 6, parts[3], 0.0)
            own = own + pltpu.roll(own, 2, 0)
            own = own + pltpu.roll(own, 4, 0)
            beyond = jnp.where(row < 4, pltpu.roll(parts[4], 4, 0), own)
            values.append(jnp.where(row < 2, pltpu.roll(parts[3], 2, 0), beyond))
        values = swap_bits(swap_lanes(values), 0, 1)
        for n in range(6):
            sum_ref[d, n // 2, pl.ds((n % 2) * 8, 8), :] = values[n]
        up_ref[d] = sum_ref[d, :, BS - 1, :]
        down_ref[d] = sum_ref[d, :, 0, :]


def decode(code):
    return lax.shift_right_logical(code, 5), lax.shift_right_logical(code, 1) & 15, code & 1


def survey(got, slots):
    return pl.pallas_call(
        survey_kernel,
        in_specs=[ANY],
        out_specs=[WHOLE, WHOLE, WHOLE, WHOLE],
        out_shape=[
            jax.ShapeDtypeStruct((2, LANES), jnp.int32),
            made(16, 3, BS, LANES),
            made(16, 3, LANES),
            made(16, 3, LANES),
        ],
        scratch_shapes=[
            buffer(16, 8, LANES),
            buffer(slots, 16, 40, LANES),
            pltpu.SMEM((2, LANES), jnp.int32),
            pltpu.SemaphoreType.DMA,
            pltpu.SemaphoreType.DMA((slots,)),
            pltpu.SemaphoreType.DMA,
        ],
        compiler_params=room(60),
    )(got)


def to_moments(f):
    f = list(f)
    for stride in (1, 3, 9):
        for n in range(27):
            if (n // stride) % 3 == 0:
                low, mid, high = f[n], f[n + stride], f[n + 2 * stride]
                both = low + high
                f[n], f[n + stride], f[n + 2 * stride] = both + mid, high - low, both
    return f


def from_moments(m):
    m = list(m)
    for stride in (1, 3, 9):
        for n in range(27):
            if (n // stride) % 3 == 0:
                zero, one, two = m[n], m[n + stride], m[n + 2 * stride]
                low, high = two - one, two + one
                m[n], m[n + stride], m[n + 2 * stride] = low, zero - (low + high), high
    return m


def equil_moments(pressure, velocity):
    x, y, z = velocity
    squares = (x * x, y * y, z * z)
    cross = {(1, 1, 0): x * y, (1, 0, 1): x * z, (0, 1, 1): y * z}
    third = pressure * (1.0 / 3.0)
    total = squares[0] + squares[1] + squares[2]
    out = [None] * 27
    for q in range(27):
        powers = (q // 9, q // 3 % 3, q % 3)
        ones = tuple(int(n == 1) for n in powers)
        scale = (1.0 / 3.0) ** sum(n == 2 for n in powers)
        if sum(ones) == 0:
            two = [squares[n] for n in range(3) if powers[n] == 2]
            value = pressure if not two else pressure + 3.0 * sum(two[1:], two[0])
            out[q] = value if scale == 1.0 else scale * value
        elif sum(ones) == 1:
            value = velocity[ones.index(1)]
            out[q] = value if scale == 1.0 else scale * value
        elif sum(ones) == 2:
            out[q] = cross[ones] if scale == 1.0 else scale * cross[ones]
        else:
            out[q] = 0.0
    return out


def weighted(v, table):
    return table[sum(map(abs, v))]


FULL_WEIGHT = [8.0 / 27.0, 2.0 / 27.0, 1.0 / 54.0, 1.0 / 216.0]
SMALL_WEIGHT = [2.0 / 9.0, 1.0 / 9.0, 0.0, 1.0 / 72.0]


def dot(v, parts):
    total = None
    for c, part in zip(v, parts):
        if c != 0:
            if total is None:
                total = part if c > 0 else -part
            else:
                total = total + part if c > 0 else total - part
    return total


def collide_kernel(
    rate_ref, code_ref, got, sums, low, high, out,
    sum_ref, low_ref, high_ref, b_ref, n_ref, o_ref, side_sem, b_sem, o_sem,
):
    place = code_ref[1, 0]
    sides = [
        pltpu.make_async_copy(a, b, side_sem.at[n])
        for n, (a, b) in enumerate(((sums, sum_ref), (low, low_ref), (high, high_ref)))
    ]

    def start(d):
        for level in range(8):
            sender, slot, _ = decode(code_ref[0, d * 8 + level])
            rows = pl.ds(pl.multiple_of(slot * SLOT_ROWS, 8), SLOT_ROWS)
            pltpu.make_async_copy(got.at[sender, rows, :], b_ref.at[d, level], b_sem.at[d]).start()

    def leave(d):
        left = jnp.where(place == 0, (d + 15) % 16, d)
        right = jnp.where(place == 15, (d + 1) % 16, d)
        for group, to in enumerate((left, d, right)):
            comps = pl.ds(group * 14, 14)
            yield pltpu.make_async_copy(o_ref.at[d, comps], out.at[to, comps], o_sem.at[d, group])

    for copy in sides:
        copy.start()
    for d in range(AHEAD):
        start(d)
    for copy in sides:
        copy.wait()

    @pl.loop(0, 16)
    def _(d):
        @pl.when(d + AHEAD < 16)
        def _():
            start(d + AHEAD)

        pltpu.make_async_copy(b_ref.at[d], b_ref.at[d], b_sem.at[d]).wait()
        for group, comps in enumerate(GROUPS):
            values = [b_ref[d, level, pl.ds(group * 8, 8), :] for level in range(8)]
            values = swap_bits(swap_lanes(values), 0, 1)
            for n in range(8):
                if comps[n // 2] < 42:
                    n_ref[comps[n // 2], pl.ds((n % 2) * 8, 8), :] = values[n]
        position = lax.broadcasted_iota(jnp.int32, (8, LANES), 1) // 16
        flag_line = jnp.zeros((8, LANES), jnp.float32)
        for level in range(8):
            flag = decode(code_ref[0, d * 8 + level])[2].astype(jnp.float32)
            flag_line = jnp.where(position == level, flag, flag_line)
        collide_plane(d, place, rate_ref, n_ref, sum_ref, low_ref, high_ref, flag_line, o_ref)
        for copy in leave(d):
            copy.start()

    for d in range(16):
        for copy in leave(d):
            copy.wait()


def collide_plane(d, place, rate_ref, n_ref, sum_ref, low_ref, high_ref, flag_line, out_ref):
    left = jnp.where(place == 0, (d + 15) % 16, d)
    right = jnp.where(place == 15, (d + 1) % 16, d)
    row = lax.broadcasted_iota(jnp.int32, (BS, LANES), 0)

    planes = []
    for index, which in ((left, 0), (d, 2), (right, 1)):
        centre = sum_ref[index, which]
        low = low_ref[index, pl.ds(which, 1), :]
        high = high_ref[index, pl.ds(which, 1), :]
        minus = jnp.where(row == 0, low, pltpu.roll(centre, 1, 0))
        plus = jnp.where(row == BS - 1, high, pltpu.roll(centre, BS - 1, 0))
        smooth_y = (2.0 / 3.0) * centre + (1.0 / 6.0) * (minus + plus)
        planes.append((smooth_y, plus - minus))

    def along_z(v):
        return pltpu.roll(v, LANES - 1, 1), pltpu.roll(v, 1, 1)

    def smooth_z(v):
        plus, minus = along_z(v)
        return (2.0 / 3.0) * v + (1.0 / 6.0) * (plus + minus)

    grad_x = 0.5 * smooth_z(planes[2][0] - planes[0][0])
    sides = planes[0][1] + planes[2][1]
    grad_y = 0.5 * smooth_z((2.0 / 3.0) * planes[1][1] + (1.0 / 6.0) * sides)
    sides = planes[0][0] + planes[2][0]
    plus, minus = along_z((2.0 / 3.0) * planes[1][0] + (1.0 / 6.0) * sides)
    grad_z = 0.5 * (plus - minus)

    for half in range(2):
        rows = slice(half * 8, half * 8 + 8)
        at = pl.ds(half * 8, 8)
        f = [n_ref[q, at, :] for q in range(27)]
        phase = sum_ref[d, 2, at, :]
        raw = to_moments(f)
        velocity = (raw[9], raw[3], raw[1])
        rest = equil_moments(raw[0], velocity)
        clipped = jnp.clip(phase, 0.0, 1.0)
        density = 0.001 + 0.999 * clipped
        dynamic = 1e-05 + 0.09999 * clipped
        shear = density / (0.5 * density + 3.0 * dynamic)
        scaled = [0.0] * 27
        for q in range(27):
            fold = 0.5 ** sum(n != 0 for n in (q // 9, q // 3 % 3, q % 3))
            rate = shear if q in (4, 10, 12) else rate_ref[q]
            scaled[q] = (rate * fold) * (raw[q] - rest[q])
        back = from_moments(scaled)

        def put(kind, index, v, value):
            out_ref[d, PLACE[kind, index], at, :] = value

        for q in range(27):
            put("h", q, FULL[q], f[q] - back[q])

        g = (grad_x[rows], grad_y[rows], grad_z[rows])
        scale = lax.rsqrt(g[0] * g[0] + g[1] * g[1] + g[2] * g[2] + 0.25)
        sharp = flag_line * (4.0 * phase * (1.0 - phase)) * scale
        drive = [3.0 * phase * velocity[n] + sharp * g[n] for n in range(3)]
        for k in range(15):
            w = weighted(SMALL[k], SMALL_WEIGHT)
            pop = n_ref[27 + k, at, :]
            push = dot(SMALL[k], drive)
            equil = w * (phase if push is None else phase + push)
            put("p", k, SMALL[k], pop - (pop - equil) * (1.0 / 0.7))


def collide(rates, code, got, sums, low, high):
    return pl.pallas_call(
        collide_kernel,
        in_specs=[SMEM, SMEM, ANY, ANY, ANY, ANY],
        out_specs=ANY,
        out_shape=made(16, 42, BS, LANES),
        scratch_shapes=[
            buffer(16, 3, BS, LANES),
            buffer(16, 3, LANES),
            buffer(16, 3, LANES),
            buffer(16, 8, SLOT_ROWS, LANES),
            buffer(42, BS, LANES),
            buffer(16, 42, BS, LANES),
            pltpu.SemaphoreType.DMA((3,)),
            pltpu.SemaphoreType.DMA((16,)),
            pltpu.SemaphoreType.DMA((16, 3)),
        ],
        compiler_params=room(60),
    )(rates, code, got, sums, low, high)


def finish_kernel(got, low, high, hydro, phase, low_ref, high_ref, n_ref, h_ref, p_ref, side_sem, n_sem, h_sem, p_sem):
    row = lax.broadcasted_iota(jnp.int32, (BS, LANES), 0)

    def load(i):
        return pltpu.make_async_copy(got.at[i], n_ref.at[i], n_sem.at[i])

    leave = []
    for part in range(4):
        copies = []
        for group in range(3):
            first = part * 4 + group - 1
            cuts = ((first, 4),)
            if first < 0:
                cuts = ((15, 1), (0, 3))
            elif first > 12:
                cuts = ((13, 3), (0, 1))
            for x, count in cuts:
                at = len(copies)
                for source, to, width, sem in ((h_ref, hydro, 9, h_sem), (p_ref, phase, 5, p_sem)):
                    box = (pl.ds(group * width, width), pl.ds(x, count))
                    copies.append(pltpu.make_async_copy(source.at[box], to.at[box], sem.at[part, at]))
        leave.append(copies)

    sides = [
        pltpu.make_async_copy(a, b, side_sem.at[n])
        for n, (a, b) in enumerate(((low, low_ref), (high, high_ref)))
    ]
    for copy in sides:
        copy.start()
    for i in range(16):
        load(i).start()
    for copy in sides:
        copy.wait()

    def plane(i):
        load(i).wait()
        for n, (kind, index, v) in enumerate(ORDER):
            value = n_ref[i, n]
            if v[1] == 1:
                face = low_ref[i, pl.ds(UP_FACE.index(n), 1), :]
                value = jnp.where(row == 0, face, pltpu.roll(value, 1, 0))
            elif v[1] == -1:
                face = high_ref[i, pl.ds(DOWN_FACE.index(n), 1), :]
                value = jnp.where(row == BS - 1, face, pltpu.roll(value, BS - 1, 0))
            if v[2] != 0:
                value = pltpu.roll(value, v[2] % LANES, 1)
            (h_ref if kind == "h" else p_ref)[index, (i + v[0]) & 15] = value

    for part in range(4):
        pl.loop(part * 4, part * 4 + 4)(plane)
        for copy in leave[part]:
            copy.start()
    for copies in leave:
        for copy in copies:
            copy.wait()


def finish(got, low, high):
    return pl.pallas_call(
        finish_kernel,
        in_specs=[ANY, ANY, ANY],
        out_specs=[ANY, ANY],
        out_shape=[made(27, BS, BS, LANES), made(15, BS, BS, LANES)],
        scratch_shapes=[
            buffer(16, 14, LANES),
            buffer(16, 14, LANES),
            buffer(16, 42, BS, LANES),
            buffer(27, BS, BS, LANES),
            buffer(15, BS, BS, LANES),
            pltpu.SemaphoreType.DMA((2,)),
            pltpu.SemaphoreType.DMA((16,)),
            pltpu.SemaphoreType.DMA((4, 8)),
            pltpu.SemaphoreType.DMA((4, 8)),
        ],
        compiler_params=room(24),
    )(got, low, high)


def swap_faces(upper, lower):
    size = lax.axis_size("gy")
    up = [(i, (i + 1) % size) for i in range(size)]
    down = [(j, i) for i, j in up]
    return lax.ppermute(upper, "gy", up), lax.ppermute(lower, "gy", down)


def on_device(hydro_old, phase_old, targets, flags, relax_rates):
    slots = targets.shape[1]
    packed = pack(hydro_old[0], phase_old[0], targets, flags)
    got = lax.all_to_all(packed, "gx", split_axis=0, concat_axis=0, tiled=True)
    code, sums, up, down = survey(got, slots)
    low, high = swap_faces(up, down)
    send = collide(relax_rates, code, got, sums, low, high)
    final = lax.all_to_all(send, "gx", split_axis=0, concat_axis=0, tiled=True)
    upper = jnp.concatenate([final[:, a:b, BS - 1, :] for a, b in runs(UP_FACE)], axis=1)
    lower = jnp.concatenate([final[:, a:b, 0, :] for a, b in runs(DOWN_FACE)], axis=1)
    low, high = swap_faces(upper, lower)
    return tuple(finish(final, low, high))


def solution(mesh):
    in_specs = (
        P("gy", "gx", None, None),
        P("gy", "gx", None, None),
        P("gy", "gx"),
        P("gy", "gx"),
        P(),
    )
    out_specs = (P(None, "gx", "gy", None), P(None, "gx", "gy", None))
    return jax.shard_map(
        on_device, mesh=mesh, in_specs=in_specs, out_specs=out_specs, check_vma=False
    )
```
